256 devices in a mesh: seq: 64 (over z, x, core), head: 4 (over y).
Axes of the slice: x: 4, y: 4, z: 8, core: 2. Of those that a mesh axis runs over, the one named last changes fastest.
Arguments:
- queries: bfloat16 [16384, 4096], P('seq', 'head'), may hold values from -6 to 6
- keys: bfloat16 [16384, 4096], P('seq', 'head'), may hold values from -6 to 6
- values: bfloat16 [16384, 4096], P('seq', 'head'), may hold values from -6 to 6
- outputs: bfloat16 [16384, 4096], P('seq', 'head'), may hold values from -6 to 6
- out_grad: bfloat16 [16384, 4096], P('seq', 'head'), may hold values from -6 to 6
- log_sum: float32 [32, 16384], P('head', 'seq'), may hold values from 4 to 6
- selected: int32 [32, 256, 16], P('head', 'seq'), may hold values from -1 to 255, as said below
- w_query: bfloat16 [4096, 4096], P(None, 'head'), may hold values from -0.09375 to 0.09375
Outputs:
- x_grad: bfloat16 [16384, 4096], P(('seq', 'head'))
- key_gradient: bfloat16 [16384, 4096], P('seq', 'head')
- value_gradient: bfloat16 [16384, 4096], P('seq', 'head')
The draws below stay inside these ranges and needn't reach their ends.
Inputs may be any that keep to these rules, and one draw needn't show every extreme that they name: Row (h, b) lists distinct blocks: entry 0 is b itself, the others are blocks before b, and entries equal to -1 (unused) come last. Over the query blocks of one index of seq and the heads of one index of head, the distinct (head, block) pairs selected from the blocks of any one other index of seq number at most 2; some pair of indices reaches 2 in every draw.
All inputs are finite; a program needn't handle non-finite values.
Results may differ from the reference program's by a relative error of at most 0.0075.
Values may be sent and summed in bfloat16 or wider, within the bound.
A program may use at most 128 MiB of HBM per device.

```python
import jax
import jax.numpy as jnp
from jax import lax

DWIN = 4096
HEADS_DEV = 8
HD = 128
BLOCK = 64
TOPK = 16
CAP = 2
BLK_DEV = 4
TOKENS = 16384
NQB = 256
HEADS = 32


def draw_selected(key, part):
    shards = NQB // BLK_DEV
    groups = HEADS // HEADS_DEV
    pick_count = TOPK - 1
    score_span = 1 << 16
    key_order, key_offset, key_pick = jax.random.split(jax.random.fold_in(key, 7), 3)
    requester = jnp.arange(shards, dtype=jnp.int32)
    ranking = jax.random.randint(key_order, (groups, shards, shards), 0, score_span) * shards + requester[None, None, :]
    ranking = jnp.where(requester[None, None, :] < requester[None, :, None], ranking, ranking + score_span * shards)
    ranking = jnp.argsort(ranking, axis=-1, stable=True).astype(jnp.int32)
    remote_count = jnp.minimum(pick_count, CAP * requester // HEADS_DEV)
    head_local = jnp.arange(HEADS_DEV, dtype=jnp.int32)
    column = jnp.arange(pick_count, dtype=jnp.int32)
    slot_number = head_local[None, :, None] * remote_count[:, None, None] + column[None, None, :]
    slot_number = jnp.minimum(slot_number, shards * CAP - 1)
    lookup = jnp.broadcast_to((slot_number // CAP).reshape(1, shards, -1), (groups, shards, HEADS_DEV * pick_count))
    source = jnp.take_along_axis(ranking, lookup, axis=2)
    offset = jax.random.randint(key_offset, (groups, shards, shards), 0, BLK_DEV)
    offset = jnp.take_along_axis(offset, source, axis=2).reshape(groups, shards, HEADS_DEV, pick_count)
    source = source.reshape(groups, shards, HEADS_DEV, pick_count)
    remote_block = source * BLK_DEV + (offset + slot_number[None] % CAP) % BLK_DEV
    remote_valid = jnp.broadcast_to((column[None, :] < remote_count[:, None])[None, :, None, :], remote_block.shape)
    inner = jnp.arange(BLK_DEV, dtype=jnp.int32)
    earlier = jnp.arange(BLK_DEV - 1, dtype=jnp.int32)
    local_block = requester[:, None, None] * BLK_DEV + earlier[None, None, :] + 0 * inner[None, :, None]
    local_valid = earlier[None, :] < inner[:, None]
    full_shape = (groups, shards, HEADS_DEV, BLK_DEV)
    candidate = jnp.concatenate((jnp.broadcast_to(remote_block[:, :, :, None, :], full_shape + (pick_count,)), jnp.broadcast_to(local_block[None, :, None, :, :], full_shape + (BLK_DEV - 1,))), axis=-1)
    usable = jnp.concatenate((jnp.broadcast_to(remote_valid[:, :, :, None, :], full_shape + (pick_count,)), jnp.broadcast_to(local_valid[None, None, None, :, :], full_shape + (BLK_DEV - 1,))), axis=-1)
    width_all = pick_count + BLK_DEV - 1
    shuffle = jax.random.randint(key_pick, candidate.shape, 0, score_span) * width_all + jnp.arange(width_all, dtype=jnp.int32)
    shuffle = jnp.where(usable, shuffle, shuffle + score_span * width_all)
    picked = jnp.argsort(shuffle, axis=-1, stable=True)[..., :pick_count]
    chosen = jnp.take_along_axis(candidate, picked, axis=-1)
    chosen_valid = jnp.take_along_axis(usable, picked, axis=-1)
    chosen = jnp.where(chosen_valid, chosen, -1)
    own_block = jnp.broadcast_to((requester[:, None] * BLK_DEV + inner[None, :])[None, :, None, :, None], full_shape + (1,))
    selection = jnp.concatenate((own_block, chosen), axis=-1)
    selection = selection.transpose(0, 2, 1, 3, 4).reshape(HEADS, NQB, TOPK)
    return selection.astype(jnp.int32)


def shard_levels(rng, shape, cuts, low, top_value):
    level = 1.0
    for axis_at, blocks in cuts:
        steps = jax.random.uniform(jax.random.fold_in(jax.random.fold_in(rng, 6), axis_at), (blocks,), jnp.float32, low / len(cuts), top_value / len(cuts))
        level = level * jnp.repeat(jnp.exp(steps), shape[axis_at] // blocks).reshape((-1,) + (1,) * (len(shape) - 1 - axis_at))
    return level


def normal_values(stream_key, extent, scale, limit, cuts=(), kind=jnp.bfloat16):
    loudness = shard_levels(stream_key, extent, cuts, -0.22, 0.18) if cuts else 1.0
    array = jax.random.normal(stream_key, extent, jnp.float32) * scale * loudness
    return jnp.minimum(jnp.maximum(array, -limit), limit).astype(kind)


def setup_inputs(seed: int = 0) -> dict:
    streams_of = jax.random.split(jax.random.key(seed), 9)
    return {
        "queries": normal_values(streams_of[0], (TOKENS, HEADS * HD), 1.0, 6.0, ((0, 64), (1, 4))),
        "keys": normal_values(streams_of[1], (TOKENS, HEADS * HD), 1.0, 6.0, ((0, 64), (1, 4))),
        "values": normal_values(streams_of[2], (TOKENS, HEADS * HD), 1.0, 6.0, ((0, 64), (1, 4))),
        "outputs": normal_values(streams_of[3], (TOKENS, HEADS * HD), 1.0, 6.0, ((0, 64), (1, 4))),
        "out_grad": normal_values(streams_of[4], (TOKENS, HEADS * HD), 1.0, 6.0, ((0, 64), (1, 4))),
        "log_sum": jnp.clip(4.0 + 2.0 * jax.random.uniform(streams_of[5], (HEADS, TOKENS), jnp.float32) ** shard_levels(streams_of[5], (HEADS, TOKENS), ((0, 4), (1, 64)), -0.2, 0.2), 4.0, 6.0),
        "selected": draw_selected(jax.random.fold_in(streams_of[8], 71), 0),
        "w_query": normal_values(streams_of[7], (DWIN, HEADS * HD), (HEADS * HD) ** -0.5, 0.09375, ((1, 4),)),
    }


def reference(queries, keys, values, outputs, out_grad, log_sum, selected, w_query):
    logit_scale = HD ** -0.5
    offsets = jnp.arange(BLOCK, dtype=jnp.int32)
    query_pos = jnp.arange(NQB, dtype=jnp.int32)[:, None] * BLOCK + offsets[None, :]

    def one_head(head_number):
        def columns(matrix):
            part = lax.dynamic_slice_in_dim(matrix, head_number * HD, HD, 1)
            return part.astype(jnp.float32).reshape(NQB, BLOCK, HD)

        query_slice = columns(queries)
        key_part = columns(keys)
        value_part = columns(values)
        partial_gradient = columns(out_grad)
        out_part = columns(outputs)
        log_part = lax.dynamic_index_in_dim(log_sum, head_number, 0, False).reshape(NQB, BLOCK)
        chosen = lax.dynamic_index_in_dim(selected, head_number, 0, False)
        safe = jnp.maximum(chosen, 0).astype(jnp.int32)
        selected_keys = key_part[safe]
        selected_values = value_part[safe]
        delta = jnp.sum(partial_gradient * out_part, axis=-1)
        attention_logits = jnp.einsum("wyj,wcmj->wycm", query_slice, selected_keys) * logit_scale
        key_pos = chosen[:, None, :, None] * BLOCK + offsets[None, None, None, :]
        allowed = (chosen >= 0)[:, None, :, None] & (key_pos <= query_pos[:, :, None, None])
        probs = jnp.where(allowed, jnp.exp(attention_logits - log_part[:, :, None, None]), jnp.float32(0.0))
        reduced_probabilities = lax.optimization_barrier(probs.astype(jnp.bfloat16)).astype(jnp.float32)
        probability_gradient = jnp.einsum("wyj,wcmj->wycm", partial_gradient, selected_values)
        score_gradient = probs * (probability_gradient - delta[:, :, None, None])
        score_gradient = lax.optimization_barrier(score_gradient.astype(jnp.bfloat16)).astype(jnp.float32)
        query_gradient = jnp.einsum("gwfp,gfpe->gwe", score_gradient, selected_keys) * logit_scale
        key_gradient = jnp.einsum("unye,unv->uyev", score_gradient, query_slice) * logit_scale
        value_gradient = jnp.einsum("unye,unv->uyev", reduced_probabilities, partial_gradient)
        both = jnp.concatenate((key_gradient, value_gradient), axis=-1)
        totals = jnp.zeros((NQB, BLOCK, 2 * HD), jnp.float32).at[safe].add(both)
        return query_gradient.astype(jnp.bfloat16), totals

    query_grads, totals = lax.map(one_head, jnp.arange(HEADS, dtype=jnp.int32))
    query_rows = query_grads.reshape(HEADS, TOKENS, HD).transpose(1, 0, 2).reshape(TOKENS, HEADS * HD)
    x_grad = jnp.dot(query_rows, w_query.T, preferred_element_type=jnp.float32).astype(jnp.bfloat16)
    arranged = totals.reshape(HEADS, TOKENS, 2 * HD).transpose(1, 0, 2)
    key_gradient = arranged[:, :, :HD].reshape(TOKENS, HEADS * HD).astype(jnp.bfloat16)
    value_gradient = arranged[:, :, HD:].reshape(TOKENS, HEADS * HD).astype(jnp.bfloat16)
    return (x_grad, key_gradient, value_gradient)
```

```python
import math

import jax
import jax.numpy as jnp
from jax import lax
from jax.sharding import Mesh
from jax.sharding import PartitionSpec as P

CAP = 2
SEQ = ("seq_0", "seq_1", "seq_2")
SEQ_HEAD = ("seq_0", "seq_1", "seq_2", "head")


def whole_of(array, axes, dim):
    if not axes:
        return array
    nearer = lax.all_gather(array, axes[-1], axis=dim, tiled=True)
    return whole_of(nearer, axes[:-1], dim)


def head_units(matrix, head_count, block_count, block_size, head_size):
    shaped = matrix.reshape(block_count, block_size, head_count, head_size)
    return shaped.transpose(2, 0, 1, 3)


def slot_table(present, slot_rank, unit_count):
    slots = jnp.arange(CAP, dtype=jnp.int32)
    matched = (present[:, None, :] == 1) & (slot_rank[:, None, :] == slots[None, :, None])
    labels = jnp.arange(1, unit_count + 1, dtype=jnp.int32)
    return jnp.sum(jnp.where(matched, labels[None, None, :], 0), axis=2) - 1


def rank_of(present):
    units = jnp.arange(present.shape[1], dtype=jnp.int32)
    before = (units[:, None] < units[None, :]).astype(jnp.float32)
    ranks = jnp.dot(present.astype(jnp.float32), before, preferred_element_type=jnp.float32)
    return ranks.astype(jnp.int32)


def pick_units(table, index):
    table_rows = table.shape[0]
    flat_index = index.reshape(-1)
    selector = (flat_index[:, None] == jnp.arange(table_rows, dtype=jnp.int32)[None, :]).astype(
        table.dtype
    )
    picked = jnp.dot(selector, table.reshape(table_rows, -1), preferred_element_type=jnp.float32)
    return picked.astype(table.dtype).reshape(index.shape + table.shape[1:])


def add_units(total, index, rows):
    total_rows = total.shape[0]
    flat_index = index.reshape(-1)
    selector = (jnp.arange(total_rows, dtype=jnp.int32)[:, None] == flat_index[None, :]).astype(
        jnp.float32
    )
    summed = jnp.dot(
        selector,
        rows.reshape(flat_index.shape[0], -1),
        preferred_element_type=jnp.float32,
        precision=lax.Precision.HIGHEST,
    )
    return total + summed.reshape(total.shape)


def attend(
    key_pool,
    pool_index,
    chosen,
    query_units,
    grad_units,
    log_units,
    delta_units,
    first_block,
    carry_init,
):
    head_count, block_count, pick_count = pool_index.shape
    block_size = query_units.shape[2]
    head_size = query_units.shape[3]
    group_size = math.gcd(head_count, max(1, 512 // (block_count * block_size)))
    group_count = head_count // group_size
    logit_scale = head_size ** (-0.5)
    offsets = jnp.arange(block_size, dtype=jnp.int32)
    query_pos = (first_block + jnp.arange(block_count, dtype=jnp.int32))[
        :, None
    ] * block_size + offsets[None, :]

    def folded(array):
        return array.reshape((group_count, group_size) + array.shape[1:])

    def step(carry, inputs):
        query_slice, partial_gradient, log_part, delta_part, index_part, chosen_part = inputs
        gathered = pick_units(key_pool, index_part)
        key_part = gathered[..., :head_size]
        value_part = gathered[..., head_size:]
        attention_logits = (
            jnp.einsum(
                "gbqd,gbksd->gbqks", query_slice, key_part, preferred_element_type=jnp.float32
            )
            * logit_scale
        )
        key_pos = chosen_part[:, :, None, :, None] * block_size + offsets
        allowed = (chosen_part >= 0)[:, :, None, :, None] & (
            key_pos <= query_pos[None, :, :, None, None]
        )
        probs = jnp.where(
            allowed, jnp.exp(attention_logits - log_part[..., None, None]), jnp.float32(0.0)
        )
        reduced_probabilities = probs.astype(jnp.bfloat16)
        probability_gradient = jnp.einsum(
            "gbqd,gbksd->gbqks", partial_gradient, value_part, preferred_element_type=jnp.float32
        )
        score_gradient = (probs * (probability_gradient - delta_part[..., None, None])).astype(
            jnp.bfloat16
        )
        query_gradient = (
            jnp.einsum(
                "gbqks,gbksd->gbqd", score_gradient, key_part, preferred_element_type=jnp.float32
            )
            * logit_scale
        )
        key_gradient = (
            jnp.einsum(
                "gbqks,gbqd->gbksd", score_gradient, query_slice, preferred_element_type=jnp.float32
            )
            * logit_scale
        )
        value_gradient = jnp.einsum(
            "gbqks,gbqd->gbksd",
            reduced_probabilities,
            partial_gradient,
            preferred_element_type=jnp.float32,
        )
        both = jnp.concatenate((key_gradient, value_gradient), axis=-1).reshape(
            -1, block_size, 2 * head_size
        )
        carry = add_units(carry, index_part, both)
        return (carry, query_gradient)

    inputs = tuple(
        (
            folded(array)
            for array in (query_units, grad_units, log_units, delta_units, pool_index, chosen)
        )
    )
    totals, query_gradient = lax.scan(step, carry_init, inputs)
    return (totals, query_gradient.reshape(query_units.shape))


def per_device(queries, keys, values, outputs, out_grad, log_sum, selected, w_query):
    tok_rows, row_width = queries.shape
    head_count, block_count, pick_count = selected.shape
    head_size = row_width // head_count
    block_size = tok_rows // block_count
    unit_count = head_count * block_count
    shard_count = lax.axis_size(SEQ)
    my_index = lax.axis_index(SEQ)
    first_block = my_index * block_count
    query_units = head_units(queries, head_count, block_count, block_size, head_size)
    grad_units = head_units(out_grad, head_count, block_count, block_size, head_size)
    local_kv = jnp.concatenate(
        (
            head_units(keys, head_count, block_count, block_size, head_size),
            head_units(values, head_count, block_count, block_size, head_size),
        ),
        axis=-1,
    )
    local_kv = local_kv.reshape(unit_count, block_size, 2 * head_size)
    products = out_grad.astype(jnp.float32) * outputs.astype(jnp.float32)
    delta_units = jnp.sum(products.reshape(tok_rows, head_count, head_size), axis=-1).T.reshape(
        head_count, block_count, block_size
    )
    log_units = log_sum.reshape(head_count, block_count, block_size)
    owner_index = selected // block_count
    local_block = selected % block_count
    remote = (selected >= 0) & (owner_index != my_index)
    all_blocks = jnp.arange(shard_count * block_count, dtype=jnp.int32)
    matches = jnp.any(
        selected.reshape(head_count, block_count * pick_count, 1) == all_blocks[None, None, :],
        axis=1,
    )
    matches = matches & (all_blocks // block_count != my_index)[None, :]
    present = matches.reshape(head_count, shard_count, block_count).transpose(1, 0, 2)
    present = present.reshape(shard_count, unit_count).astype(jnp.int32)
    slot_rank = rank_of(present)
    head_column = jnp.arange(head_count, dtype=jnp.int32)[:, None, None] * block_count
    owner_safe = jnp.clip(owner_index, 0, shard_count - 1)
    rank_at = slot_rank.reshape(-1)[owner_safe * unit_count + head_column + local_block]
    pool_index = jnp.where(
        remote, unit_count + owner_safe * CAP + rank_at, head_column + local_block
    )
    everyone = whole_of(selected, SEQ, 1)
    mine = first_block + jnp.arange(block_count, dtype=jnp.int32)
    asked = jnp.any(
        everyone.reshape(head_count, shard_count, block_count * pick_count, 1) == mine, axis=2
    )
    asked = asked & (jnp.arange(shard_count) != my_index)[None, :, None]
    present_in = asked.transpose(1, 0, 2).reshape(shard_count, unit_count).astype(jnp.int32)
    incoming = slot_table(present_in, rank_of(present_in), unit_count)
    outgoing = pick_units(local_kv, incoming)
    zero_grads = jnp.zeros((unit_count, block_size, 2 * head_size), jnp.float32)
    remote_zero = jnp.zeros((shard_count * CAP, block_size, 2 * head_size), jnp.float32)
    early_grads, early_query = attend(
        local_kv,
        pool_index[:, :, :1],
        selected[:, :, :1],
        query_units,
        grad_units,
        log_units,
        delta_units,
        first_block,
        zero_grads,
    )
    pulled = lax.all_to_all(outgoing, SEQ, split_axis=0, concat_axis=0, tiled=True)
    key_pool = jnp.concatenate(
        (local_kv, pulled.reshape(shard_count * CAP, block_size, 2 * head_size)), axis=0
    )
    pool_grads, late_query = attend(
        key_pool,
        pool_index[:, :, 1:],
        selected[:, :, 1:],
        query_units,
        grad_units,
        log_units,
        delta_units,
        first_block,
        jnp.concatenate((early_grads, remote_zero), axis=0),
    )
    query_gradient = early_query + late_query
    returned = lax.all_to_all(
        pool_grads[unit_count:]
        .reshape(shard_count, CAP, block_size, 2 * head_size)
        .astype(jnp.bfloat16),
        SEQ,
        split_axis=0,
        concat_axis=0,
        tiled=True,
    ).astype(jnp.float32)
    own_grads = pool_grads[:unit_count]
    local_grads = add_units(own_grads, incoming, returned.reshape(-1, block_size, 2 * head_size))
    arranged = local_grads.reshape(head_count, block_count, block_size, 2 * head_size).transpose(
        1, 2, 0, 3
    )
    key_gradient = arranged[..., :head_size].reshape(tok_rows, row_width).astype(jnp.bfloat16)
    value_gradient = arranged[..., head_size:].reshape(tok_rows, row_width).astype(jnp.bfloat16)
    query_rows = (
        query_gradient.astype(jnp.bfloat16).transpose(1, 2, 0, 3).reshape(tok_rows, row_width)
    )
    x_grad = lax.psum_scatter(
        lax.dot_general(
            query_rows, w_query, (((1,), (1,)), ((), ())), preferred_element_type=jnp.float32
        ),
        "head",
        scatter_dimension=0,
        tiled=True,
    ).astype(jnp.bfloat16)
    return (x_grad, key_gradient, value_gradient)


def solution(mesh):
    finer = Mesh(
        mesh.devices.reshape(8, 4, 2, mesh.shape["head"]), ("seq_0", "seq_1", "seq_2", "head")
    )
    in_specs = (
        P(SEQ, "head"),
        P(SEQ, "head"),
        P(SEQ, "head"),
        P(SEQ, "head"),
        P(SEQ, "head"),
        P("head", SEQ),
        P("head", SEQ, None),
        P(None, "head"),
    )
    out_specs = (P(SEQ_HEAD, None), P(SEQ, "head"), P(SEQ, "head"))
    return jax.shard_map(
        per_device, mesh=finer, in_specs=in_specs, out_specs=out_specs, check_vma=False
    )
```

```python
import functools

import jax
import jax.numpy as jnp
from jax import lax
from jax.experimental import pallas as pl
from jax.experimental.pallas import tpu as pltpu
from jax.sharding import PartitionSpec as P

CAP = 2
HD = 128
BLOCK = 64
FAR = 1e30

NT = (((1,), (1,)), ((), ()))
TN = (((0,), (0,)), ((), ()))


def dot(a, b, dims=(((1,), (0,)), ((), ()))):
    return lax.dot_general(a, b, dims, preferred_element_type=jnp.float32)


def request_tables(selected, me, shards):
    heads, blocks, picks = selected.shape
    units = heads * blocks
    every = jnp.arange(shards * blocks, dtype=jnp.int32)
    hit = jnp.any(selected[:, :, :, None] == every, axis=2)
    weight = (1 << jnp.arange(blocks, dtype=jnp.int32))[None, :, None]
    bits = jnp.sum(jnp.where(hit, weight, 0), axis=1)
    bits = bits.reshape(heads, shards, blocks).transpose(1, 0, 2).reshape(shards, units)
    owners = jnp.arange(shards, dtype=jnp.int32)[:, None]
    local = jnp.sum(jnp.where(owners == me, bits, 0), axis=0)
    bits = jnp.where(owners == me, 0, bits)
    index = jnp.arange(units, dtype=jnp.int32)
    first = jnp.min(jnp.where(bits > 0, index, units), axis=1, keepdims=True)
    second = jnp.min(jnp.where((bits > 0) & (index > first), index, units), axis=1, keepdims=True)
    unit = jnp.concatenate((first, second), axis=1)
    mask = jnp.sum(jnp.where(unit[:, :, None] == index, bits[:, None, :], 0), axis=2)
    return jnp.where(unit == units, -1, unit), mask, local


def unit_place(unit, blocks):
    head = unit // blocks
    return (
        pl.ds(pl.multiple_of((unit - head * blocks) * BLOCK, BLOCK), BLOCK),
        pl.ds(pl.multiple_of(head * HD, HD), HD),
    )


def pack_kernel(blocks, asked, keys, values, out):
    def body(slot, _):
        @pl.when(asked[slot] >= 0)
        def _():
            rows, cols = unit_place(asked[slot], blocks)
            out[slot, :, :HD] = keys[rows, cols]
            out[slot, :, HD:] = values[rows, cols]

        return 0

    lax.fori_loop(0, out.shape[0], body, 0)


def backward(key, value, query, grad, log_row, delta_row, allowed=None):
    scale = HD**-0.5
    probs = jnp.exp(dot(key, query, NT) * scale - log_row)
    if allowed is not None:
        probs = jnp.where(allowed, probs, 0.0)
    dscores = (probs * (dot(value, grad, NT) - delta_row)).astype(jnp.bfloat16)
    return dot(key, dscores, TN), dot(dscores, query) * scale, dot(probs.astype(jnp.bfloat16), grad)


def attend_kernel(
    unit, mask, local, queries, keys, values, grads, logs, deltas, pulled, back, dqt, dk, dv, total
):
    heads = logs.shape[0]
    tokens = queries.shape[0]
    blocks = tokens // BLOCK
    lane_block = lax.broadcasted_iota(jnp.int32, (1, tokens), 1) // BLOCK

    def open_logs(head, bits):
        return jnp.where(((bits >> lane_block) & 1) == 1, logs[head], FAR)

    def one_head(head, _):
        cols = pl.ds(pl.multiple_of(head * HD, HD), HD)
        query, grad = queries[:, cols], grads[:, cols]
        rows = lax.broadcasted_iota(jnp.int32, (BLOCK, tokens), 0)
        lanes = lax.broadcasted_iota(jnp.int32, (BLOCK, tokens), 1)
        sums = jnp.zeros((HD, tokens), jnp.float32)
        for block in range(blocks):
            place = slice(block * BLOCK, (block + 1) * BLOCK)
            dq, dk_part, dv_part = backward(
                keys[place, cols],
                values[place, cols],
                query,
                grad,
                open_logs(head, local[head * blocks + block]),
                deltas[head],
                rows + block * BLOCK <= lanes,
            )
            sums += dq
            dk[place, cols] = dk_part
            dv[place, cols] = dv_part
        total[head] = sums
        return 0

    lax.fori_loop(0, heads, one_head, 0)

    def one_slot(slot, _):
        @pl.when(unit[slot] >= 0)
        def _():
            head = unit[slot] // blocks
            cols = pl.ds(pl.multiple_of(head * HD, HD), HD)
            dq, dk_part, dv_part = backward(
                pulled[slot, :, :HD],
                pulled[slot, :, HD:],
                queries[:, cols],
                grads[:, cols],
                open_logs(head, mask[slot]),
                deltas[head],
            )
            total[head] += dq
            back[slot, :, :HD] = dk_part.astype(jnp.bfloat16)
            back[slot, :, HD:] = dv_part.astype(jnp.bfloat16)

        return 0

    lax.fori_loop(0, pulled.shape[0], one_slot, 0)
    dqt[...] = (total[...] * HD**-0.5).astype(jnp.bfloat16)


def settle_kernel(blocks, asked, returned, dk, dv, dk_out, dv_out, dk_sum, dv_sum):
    dk_sum[...] = dk[...]
    dv_sum[...] = dv[...]

    def body(slot, _):
        @pl.when(asked[slot] >= 0)
        def _():
            rows, cols = unit_place(asked[slot], blocks)
            dk_sum[rows, cols] += returned[slot, :, :HD].astype(jnp.float32)
            dv_sum[rows, cols] += returned[slot, :, HD:].astype(jnp.float32)

        return 0

    lax.fori_loop(0, returned.shape[0], body, 0)
    dk_out[...] = dk_sum[...].astype(jnp.bfloat16)
    dv_out[...] = dv_sum[...].astype(jnp.bfloat16)


SMEM = pl.BlockSpec(memory_space=pltpu.SMEM)
VMEM = pl.BlockSpec(memory_space=pltpu.VMEM)
LIMIT = pltpu.CompilerParams(vmem_limit_bytes=48 * 2**20)


def per_device(queries, keys, values, outputs, out_grad, log_sum, selected, w_query):
    tokens, width = queries.shape
    heads, blocks, _ = selected.shape
    shards = lax.axis_size("seq")
    me = lax.axis_index("seq")
    slots = shards * CAP
    low = jax.ShapeDtypeStruct((slots, BLOCK, 2 * HD), jnp.bfloat16)
    unit, mask, local = request_tables(selected, me, shards)
    asked = lax.all_to_all(unit, "seq", split_axis=0, concat_axis=0, tiled=True).reshape(-1)
    outgoing = pl.pallas_call(
        functools.partial(pack_kernel, blocks),
        out_shape=low,
        in_specs=[SMEM, VMEM, VMEM],
        out_specs=VMEM,
        compiler_params=LIMIT,
        name="pack",
    )(asked, keys, values)
    pulled = lax.all_to_all(
        outgoing.reshape(shards, CAP, BLOCK, 2 * HD), "seq", split_axis=0, concat_axis=0, tiled=True
    ).reshape(slots, BLOCK, 2 * HD)
    products = out_grad.astype(jnp.float32) * outputs.astype(jnp.float32)
    delta = jnp.sum(products.reshape(tokens, heads, HD), axis=-1).T
    wide = jax.ShapeDtypeStruct((tokens, width), jnp.float32)
    back, dqt, dk, dv = pl.pallas_call(
        attend_kernel,
        out_shape=(low, jax.ShapeDtypeStruct((heads, HD, tokens), jnp.bfloat16), wide, wide),
        in_specs=[SMEM] * 3 + [VMEM] * 7,
        out_specs=(VMEM,) * 4,
        scratch_shapes=[pltpu.VMEM((heads, HD, tokens), jnp.float32)],
        compiler_params=LIMIT,
        name="attend",
    )(
        unit.reshape(-1),
        mask.reshape(-1),
        local,
        queries,
        keys,
        values,
        out_grad,
        log_sum[:, None, :],
        delta[:, None, :],
        pulled,
    )
    returned = lax.all_to_all(
        back.reshape(shards, CAP, BLOCK, 2 * HD), "seq", split_axis=0, concat_axis=0, tiled=True
    ).reshape(slots, BLOCK, 2 * HD)
    result = jax.ShapeDtypeStruct((tokens, width), jnp.bfloat16)
    key_gradient, value_gradient = pl.pallas_call(
        functools.partial(settle_kernel, blocks),
        out_shape=(result, result),
        in_specs=[SMEM] + [VMEM] * 3,
        out_specs=(VMEM, VMEM),
        scratch_shapes=[pltpu.VMEM((tokens, width), jnp.float32)] * 2,
        compiler_params=LIMIT,
        name="settle",
    )(asked, returned, dk, dv)
    x_grad = lax.psum_scatter(
        dot(dqt.reshape(width, tokens), w_query, (((0,), (1,)), ((), ()))),
        "head",
        scatter_dimension=0,
        tiled=True,
    ).astype(jnp.bfloat16)
    return x_grad, key_gradient, value_gradient


def solution(mesh):
    in_specs = (P("seq", "head"),) * 5 + (P("head", "seq"), P("head", "seq", None), P(None, "head"))
    out_specs = (P(("seq", "head"), None), P("seq", "head"), P("seq", "head"))
    return jax.shard_map(
        per_device, mesh=mesh, in_specs=in_specs, out_specs=out_specs, check_vma=False
    )
```

```python
import functools

import jax
import jax.numpy as jnp
from jax import lax
from jax.experimental import pallas as pl
from jax.experimental.pallas import tpu as pltpu
from jax.sharding import PartitionSpec as P

CAP = 2
HD = 128
BLOCK = 64
FAR = 1e30

NT = (((1,), (1,)), ((), ()))
TN = (((0,), (0,)), ((), ()))


def dot(a, b, dims=(((1,), (0,)), ((), ()))):
    return lax.dot_general(a, b, dims, preferred_element_type=jnp.float32)


def request_tables(selected, me, shards):
    heads, blocks, picks = selected.shape
    units = heads * blocks
    every = jnp.arange(shards * blocks, dtype=jnp.int32)
    hit = jnp.any(selected[:, :, :, None] == every, axis=2)
    weight = (1 << jnp.arange(blocks, dtype=jnp.int32))[None, :, None]
    bits = jnp.sum(jnp.where(hit, weight, 0), axis=1)
    bits = bits.reshape(heads, shards, blocks).transpose(1, 0, 2).reshape(shards, units)
    owners = jnp.arange(shards, dtype=jnp.int32)[:, None]
    local = jnp.sum(jnp.where(owners == me, bits, 0), axis=0)
    bits = jnp.where(owners == me, 0, bits)
    index = jnp.arange(units, dtype=jnp.int32)
    first = jnp.min(jnp.where(bits > 0, index, units), axis=1, keepdims=True)
    second = jnp.min(jnp.where((bits > 0) & (index > first), index, units), axis=1, keepdims=True)
    unit = jnp.concatenate((first, second), axis=1)
    mask = jnp.sum(jnp.where(unit[:, :, None] == index, bits[:, None, :], 0), axis=2)
    return jnp.where(unit == units, -1, unit), mask, local


def unit_place(unit, blocks):
    head = unit // blocks
    return (
        pl.ds(pl.multiple_of((unit - head * blocks) * BLOCK, BLOCK), BLOCK),
        pl.ds(pl.multiple_of(head * HD, HD), HD),
    )


def pack_kernel(blocks, asked, keys, values, out):
    def body(slot, _):
        @pl.when(asked[slot] >= 0)
        def _():
            rows, cols = unit_place(asked[slot], blocks)
            out[slot, :, :HD] = keys[rows, cols]
            out[slot, :, HD:] = values[rows, cols]

        @pl.when(asked[slot] < 0)
        def _():
            out[slot] = jnp.zeros(out.shape[1:], out.dtype)

        return 0

    lax.fori_loop(0, out.shape[0], body, 0)


def backward(key, value, query, grad, log_row, delta_row, allowed=None):
    scale = HD**-0.5
    probs = jnp.exp(dot(key, query, NT) * scale - log_row)
    if allowed is not None:
        probs = jnp.where(allowed, probs, 0.0)
    dscores = (probs * (dot(value, grad, NT) - delta_row)).astype(jnp.bfloat16)
    return dot(key, dscores, TN), dot(dscores, query) * scale, dot(probs.astype(jnp.bfloat16), grad)


def exchange_kernel(
    picked,
    mask,
    local,
    queries,
    keys,
    values,
    grads,
    logs,
    deltas,
    outgoing,
    dqt,
    dk,
    dv,
    returned,
    pulled,
    back,
    total,
    query_heads,
    grad_heads,
    pull_send,
    pull_recv,
    back_send,
    back_recv,
):
    me = lax.axis_index("seq")
    shards = outgoing.shape[0]
    heads = logs.shape[0]
    tokens = queries.shape[0]
    blocks = tokens // BLOCK
    lane_block = lax.broadcasted_iota(jnp.int32, (1, tokens), 1) // BLOCK

    def pull_copy(slot_from, slot_to, target, index):
        return pltpu.make_async_remote_copy(
            src_ref=outgoing.at[slot_from],
            dst_ref=pulled.at[slot_to],
            send_sem=pull_send.at[slot_from],
            recv_sem=pull_recv.at[index],
            device_id={"seq": target},
            device_id_type=pl.DeviceIdType.MESH,
        )

    def back_copy(slot_from, slot_to, target, index):
        return pltpu.make_async_remote_copy(
            src_ref=back.at[slot_from],
            dst_ref=returned.at[slot_to],
            send_sem=back_send.at[slot_from],
            recv_sem=back_recv.at[index],
            device_id={"seq": target},
            device_id_type=pl.DeviceIdType.MESH,
        )

    barrier = pltpu.get_barrier_semaphore()

    def greet(step, _):
        pl.semaphore_signal(
            barrier,
            inc=1,
            device_id={"seq": lax.rem(me + step, shards)},
            device_id_type=pl.DeviceIdType.MESH,
        )
        return 0

    lax.fori_loop(1, shards, greet, 0)
    pl.semaphore_wait(barrier, shards - 1)

    def send(target, _):
        pull_copy(target, me, target, me).start()
        return 0

    lax.fori_loop(me + 1, shards, send, 0)
    for head in range(heads):
        cols = slice(head * HD, (head + 1) * HD)
        query_heads[head] = queries[:, cols]
        grad_heads[head] = grads[:, cols]

    def open_logs(head, bits):
        return jnp.where(((bits >> lane_block) & 1) == 1, logs[head], FAR)

    def one_head(head, _):
        cols = pl.ds(pl.multiple_of(head * HD, HD), HD)
        query, grad = query_heads[head], grad_heads[head]
        rows = lax.broadcasted_iota(jnp.int32, (BLOCK, tokens), 0)
        lanes = lax.broadcasted_iota(jnp.int32, (BLOCK, tokens), 1)
        sums = jnp.zeros((HD, tokens), jnp.float32)
        for block in range(blocks):
            place = slice(block * BLOCK, (block + 1) * BLOCK)
            dq, dk_part, dv_part = backward(
                keys[place, cols],
                values[place, cols],
                query,
                grad,
                open_logs(head, local[head * blocks + block]),
                deltas[head],
                rows + block * BLOCK <= lanes,
            )
            sums += dq
            dk[place, cols] = dk_part
            dv[place, cols] = dv_part
        total[head] = sums
        return 0

    lax.fori_loop(0, heads, one_head, 0)

    def one_source(step, _):
        source = me - step
        pull_copy(source, source, source, source).wait_recv()
        parts = []
        for slot in range(CAP):
            head = picked[source * CAP + slot]
            dq, dk_part, dv_part = backward(
                pulled[source, slot, :, :HD],
                pulled[source, slot, :, HD:],
                query_heads[head],
                grad_heads[head],
                open_logs(head, mask[source * CAP + slot]),
                deltas[head],
            )
            back[source, slot, :, :HD] = dk_part.astype(jnp.bfloat16)
            back[source, slot, :, HD:] = dv_part.astype(jnp.bfloat16)
            parts.append((head, dq))
        back_copy(source, me, source, me).start()
        for head in range(heads):
            total[head] += sum(
                jnp.where(jnp.full(dq.shape, at, jnp.int32) == head, dq, 0.0) for at, dq in parts
            )
        return 0

    lax.fori_loop(1, me + 1, one_source, 0)
    dqt[...] = (total[...] * HD**-0.5).astype(jnp.bfloat16)

    def finish_owner(target, _):
        pull_copy(target, target, target, target).wait_send()
        back_copy(target, target, target, target).wait_recv()
        return 0

    lax.fori_loop(me + 1, shards, finish_owner, 0)

    def finish_requester(source, _):
        back_copy(source, source, source, source).wait_send()
        return 0

    lax.fori_loop(0, me, finish_requester, 0)


def settle_kernel(blocks, asked, returned, dk, dv, dk_out, dv_out, dk_sum, dv_sum):
    dk_sum[...] = dk[...]
    dv_sum[...] = dv[...]

    def body(slot, _):
        @pl.when(asked[slot] >= 0)
        def _():
            rows, cols = unit_place(asked[slot], blocks)
            dk_sum[rows, cols] += returned[slot, :, :HD].astype(jnp.float32)
            dv_sum[rows, cols] += returned[slot, :, HD:].astype(jnp.float32)

        return 0

    lax.fori_loop(0, returned.shape[0], body, 0)
    dk_out[...] = dk_sum[...].astype(jnp.bfloat16)
    dv_out[...] = dv_sum[...].astype(jnp.bfloat16)


SMEM = pl.BlockSpec(memory_space=pltpu.SMEM)
VMEM = pl.BlockSpec(memory_space=pltpu.VMEM)
LIMIT = pltpu.CompilerParams(vmem_limit_bytes=48 * 2**20)


def per_device(queries, keys, values, outputs, out_grad, log_sum, selected, w_query):
    tokens, width = queries.shape
    heads, blocks, _ = selected.shape
    shards = lax.axis_size("seq")
    me = lax.axis_index("seq")
    slots = shards * CAP
    low = jax.ShapeDtypeStruct((slots, BLOCK, 2 * HD), jnp.bfloat16)
    unit, mask, local = request_tables(selected, me, shards)
    asked = lax.all_to_all(unit, "seq", split_axis=0, concat_axis=0, tiled=True).reshape(-1)
    outgoing = pl.pallas_call(
        functools.partial(pack_kernel, blocks),
        out_shape=low,
        in_specs=[SMEM, VMEM, VMEM],
        out_specs=VMEM,
        compiler_params=LIMIT,
        name="pack",
    )(asked, keys, values)
    products = out_grad.astype(jnp.float32) * outputs.astype(jnp.float32)
    delta = jnp.sum(products.reshape(tokens, heads, HD), axis=-1).T
    wide = jax.ShapeDtypeStruct((tokens, width), jnp.float32)
    paired = (shards, CAP, BLOCK, 2 * HD)
    dqt, dk, dv, returned = pl.pallas_call(
        exchange_kernel,
        out_shape=(
            jax.ShapeDtypeStruct((heads, HD, tokens), jnp.bfloat16),
            wide,
            wide,
            jax.ShapeDtypeStruct(paired, jnp.bfloat16),
        ),
        in_specs=[SMEM] * 3 + [VMEM] * 7,
        out_specs=(VMEM,) * 4,
        scratch_shapes=[
            pltpu.VMEM(paired, jnp.bfloat16),
            pltpu.VMEM(paired, jnp.bfloat16),
            pltpu.VMEM((heads, HD, tokens), jnp.float32),
            pltpu.VMEM((heads, tokens, HD), jnp.bfloat16),
            pltpu.VMEM((heads, tokens, HD), jnp.bfloat16),
        ]
        + [pltpu.SemaphoreType.DMA((shards,))] * 4,
        compiler_params=pltpu.CompilerParams(
            vmem_limit_bytes=48 * 2**20, collective_id=0, has_side_effects=True
        ),
        name="exchange",
    )(
        jnp.maximum(unit.reshape(-1), 0) // blocks,
        mask.reshape(-1),
        local,
        queries,
        keys,
        values,
        out_grad,
        log_sum[:, None, :],
        delta[:, None, :],
        outgoing.reshape(paired),
    )
    returned = returned.reshape(slots, BLOCK, 2 * HD)
    result = jax.ShapeDtypeStruct((tokens, width), jnp.bfloat16)
    key_gradient, value_gradient = pl.pallas_call(
        functools.partial(settle_kernel, blocks),
        out_shape=(result, result),
        in_specs=[SMEM] + [VMEM] * 3,
        out_specs=(VMEM, VMEM),
        scratch_shapes=[pltpu.VMEM((tokens, width), jnp.float32)] * 2,
        compiler_params=LIMIT,
        name="settle",
    )(asked, returned, dk, dv)
    x_grad = lax.psum_scatter(
        dot(dqt.reshape(width, tokens), w_query, (((0,), (1,)), ((), ()))),
        "head",
        scatter_dimension=0,
        tiled=True,
    ).astype(jnp.bfloat16)
    return x_grad, key_gradient, value_gradient


def solution(mesh):
    in_specs = (P("seq", "head"),) * 5 + (P("head", "seq"), P("head", "seq", None), P(None, "head"))
    out_specs = (P(("seq", "head"), None), P("seq", "head"), P("seq", "head"))
    return jax.shard_map(
        per_device, mesh=mesh, in_specs=in_specs, out_specs=out_specs, check_vma=False
    )
```

```python
import functools

import jax
import jax.numpy as jnp
from jax import lax
from jax.experimental import pallas as pl
from jax.experimental.pallas import tpu as pltpu
from jax.sharding import PartitionSpec as P

CAP = 2
HD = 128
BLOCK = 64
FAR = 1e30

NT = (((1,), (1,)), ((), ()))
TN = (((0,), (0,)), ((), ()))


def dot(a, b, dims=(((1,), (0,)), ((), ()))):
    return lax.dot_general(a, b, dims, preferred_element_type=jnp.float32)


def request_tables(selected, me, shards):
    heads, blocks, picks = selected.shape
    units = heads * blocks
    every = jnp.arange(shards * blocks, dtype=jnp.int32)
    hit = jnp.any(selected[:, :, :, None] == every, axis=2)
    weight = (1 << jnp.arange(blocks, dtype=jnp.int32))[None, :, None]
    bits = jnp.sum(jnp.where(hit, weight, 0), axis=1)
    bits = bits.reshape(heads, shards, blocks).transpose(1, 0, 2).reshape(shards, units)
    owners = jnp.arange(shards, dtype=jnp.int32)[:, None]
    local = jnp.sum(jnp.where(owners == me, bits, 0), axis=0)
    bits = jnp.where(owners == me, 0, bits)
    index = jnp.arange(units, dtype=jnp.int32)
    first = jnp.min(jnp.where(bits > 0, index, units), axis=1, keepdims=True)
    second = jnp.min(jnp.where((bits > 0) & (index > first), index, units), axis=1, keepdims=True)
    unit = jnp.concatenate((first, second), axis=1)
    mask = jnp.sum(jnp.where(unit[:, :, None] == index, bits[:, None, :], 0), axis=2)
    return jnp.where(unit == units, -1, unit), mask, local


def unit_place(unit, blocks):
    head = unit // blocks
    return (
        pl.ds(pl.multiple_of((unit - head * blocks) * BLOCK, BLOCK), BLOCK),
        pl.ds(pl.multiple_of(head * HD, HD), HD),
    )


def backward(key, value, query, grad, log_row, delta_row, allowed=None):
    scale = HD**-0.5
    probs = jnp.exp(dot(key, query, NT) * scale - log_row)
    if allowed is not None:
        probs = jnp.where(allowed, probs, 0.0)
    dscores = (probs * (dot(value, grad, NT) - delta_row)).astype(jnp.bfloat16)
    return dot(key, dscores, TN), dot(dscores, query) * scale, dot(probs.astype(jnp.bfloat16), grad)


def offset_of(step, shards):
    return lax.rem(step * 27, shards)


def exchange_kernel(
    picked,
    mask,
    local,
    queries,
    keys,
    values,
    grads,
    logs,
    deltas,
    asking,
    weight,
    x_grad,
    dk,
    dv,
    returned,
    asked,
    outgoing,
    units_here,
    asked_here,
    pulled,
    back,
    total,
    query_heads,
    grad_heads,
    weight_here,
    dq_rows,
    parts_out,
    parts_in,
    own_part,
    pull_send,
    pull_recv,
    back_send,
    back_recv,
    part_send,
    part_recv,
    ask_send,
    ask_recv,
    weight_sem,
    asked_sem,
):
    me = lax.axis_index("seq")
    lane = lax.axis_index("head")
    lanes_all = parts_out.shape[1]
    stripe, piece = parts_out.shape[2:]
    pieces = parts_out.shape[0]
    weight_copy = pltpu.make_async_copy(weight, weight_here, weight_sem)
    weight_copy.start()
    asked[...] = jnp.full(asked.shape, -1, jnp.int32)
    shards = asking.shape[0]
    heads = logs.shape[0]
    tokens = queries.shape[0]
    blocks = tokens // BLOCK
    lane_block = lax.broadcasted_iota(jnp.int32, (1, tokens), 1) // BLOCK

    def pull_copy(slot_from, slot_to, target, index):
        return pltpu.make_async_remote_copy(
            src_ref=outgoing.at[slot_from],
            dst_ref=pulled.at[slot_to],
            send_sem=pull_send.at[slot_from],
            recv_sem=pull_recv.at[index],
            device_id={"seq": target},
            device_id_type=pl.DeviceIdType.MESH,
        )

    def back_copy(slot_from, slot_to, target, index):
        return pltpu.make_async_remote_copy(
            src_ref=back.at[slot_from],
            dst_ref=returned.at[slot_to],
            send_sem=back_send.at[slot_from],
            recv_sem=back_recv.at[index],
            device_id={"seq": target},
            device_id_type=pl.DeviceIdType.MESH,
        )

    def ask_copy(slot_from, slot_to, target, index):
        return pltpu.make_async_remote_copy(
            src_ref=asking.at[slot_from],
            dst_ref=asked.at[slot_to],
            send_sem=ask_send.at[slot_from],
            recv_sem=ask_recv.at[index],
            device_id={"seq": target},
            device_id_type=pl.DeviceIdType.MESH,
        )

    def part_copy(at, slot_from, slot_to, target, index):
        return pltpu.make_async_remote_copy(
            src_ref=parts_out.at[at, slot_from],
            dst_ref=parts_in.at[at, slot_to],
            send_sem=part_send.at[at, slot_from],
            recv_sem=part_recv.at[at, index],
            device_id={"head": target},
            device_id_type=pl.DeviceIdType.MESH,
        )

    barrier = pltpu.get_barrier_semaphore()

    def greet(step, _):
        pl.semaphore_signal(
            barrier,
            inc=1,
            device_id={"seq": lax.rem(me + step, shards)},
            device_id_type=pl.DeviceIdType.MESH,
        )
        return 0

    lax.fori_loop(1, shards, greet, 0)
    for step in range(1, lanes_all):
        pl.semaphore_signal(
            barrier,
            inc=1,
            device_id={"head": lax.rem(lane + step, lanes_all)},
            device_id_type=pl.DeviceIdType.MESH,
        )
    pl.semaphore_wait(barrier, shards - 1 + lanes_all - 1)

    def ask(source, _):
        ask_copy(source, me, source, me).start()
        return 0

    lax.fori_loop(0, me, ask, 0)
    for head in range(heads):
        cols = slice(head * HD, (head + 1) * HD)
        query_heads[head] = queries[:, cols]
        grad_heads[head] = grads[:, cols]
        for block in range(blocks):
            rows = slice(block * BLOCK, (block + 1) * BLOCK)
            units_here[head * blocks + block, :, :HD] = keys[rows, cols]
            units_here[head * blocks + block, :, HD:] = values[rows, cols]

    def heard(target, _):
        ask_copy(target, target, target, target).wait_recv()
        return 0

    lax.fori_loop(me + 1, shards, heard, 0)
    asked_copy = pltpu.make_async_copy(asked, asked_here, asked_sem)
    asked_copy.start()
    asked_copy.wait()

    def send(target):
        for slot in range(CAP):
            wanted = asked_here[target, 0, slot]
            found = units_here[jnp.maximum(wanted, 0)]
            outgoing[target, slot] = jnp.where(
                jnp.full(found.shape, wanted, jnp.int32) >= 0, found, jnp.zeros_like(found)
            )
        pull_copy(target, me, target, me).start()

    def send_step(step, _):
        target = me + offset_of(step, shards)

        @pl.when(target < shards)
        def _():
            send(target)

        return 0

    lax.fori_loop(1, shards, send_step, 0)

    def open_logs(head, bits):
        return jnp.where(((bits >> lane_block) & 1) == 1, logs[head], FAR)

    def one_head(head, _):
        cols = pl.ds(pl.multiple_of(head * HD, HD), HD)
        query, grad = query_heads[head], grad_heads[head]
        rows = lax.broadcasted_iota(jnp.int32, (BLOCK, tokens), 0)
        lanes = lax.broadcasted_iota(jnp.int32, (BLOCK, tokens), 1)
        sums = jnp.zeros((HD, tokens), jnp.float32)
        for block in range(blocks):
            place = slice(block * BLOCK, (block + 1) * BLOCK)
            dq, dk_part, dv_part = backward(
                keys[place, cols],
                values[place, cols],
                query,
                grad,
                open_logs(head, local[head * blocks + block]),
                deltas[head],
                rows + block * BLOCK <= lanes,
            )
            sums += dq
            dk[place, cols] = dk_part
            dv[place, cols] = dv_part
        total[head] = sums
        return 0

    lax.fori_loop(0, heads, one_head, 0)

    def one_source(step, _):
        source = me - step
        pull_copy(source, source, source, source).wait_recv()
        parts = []
        for slot in range(CAP):
            head = picked[source * CAP + slot]
            dq, dk_part, dv_part = backward(
                pulled[source, slot, :, :HD],
                pulled[source, slot, :, HD:],
                query_heads[head],
                grad_heads[head],
                open_logs(head, mask[source * CAP + slot]),
                deltas[head],
            )
            back[source, slot, :, :HD] = dk_part.astype(jnp.bfloat16)
            back[source, slot, :, HD:] = dv_part.astype(jnp.bfloat16)
            parts.append((head, dq))
        back_copy(source, me, source, me).start()
        for head in range(heads):
            total[head] += sum(
                jnp.where(jnp.full(dq.shape, at, jnp.int32) == head, dq, 0.0) for at, dq in parts
            )
        return 0

    def source_step(step, _):
        offset = offset_of(step, shards)

        @pl.when(offset <= me)
        def _():
            one_source(offset, 0)

        return 0

    lax.fori_loop(1, shards, source_step, 0)
    for head in range(heads):
        dq_rows[:, head * HD : (head + 1) * HD] = (total[head] * HD**-0.5).T.astype(jnp.bfloat16)
    weight_copy.wait()

    def one_piece(at, _):
        columns = pl.ds(pl.multiple_of(at * piece, piece), piece)
        product = dot(dq_rows[...], weight_here[columns, :], NT).reshape(lanes_all, stripe, piece)
        own_part[at] = product
        parts_out[at] = product.astype(jnp.bfloat16)
        for step in range(1, lanes_all):
            target = lax.rem(lane + step, lanes_all)
            part_copy(at, target, lane, target, lane).start()
        return 0

    lax.fori_loop(0, pieces, one_piece, 0)

    def one_sum(at, _):
        row_sum = own_part[at, lane]
        for step in range(1, lanes_all):
            source = lax.rem(lane + step, lanes_all)
            part_copy(at, source, source, source, source).wait()
            row_sum += parts_in[at, source].astype(jnp.float32)
        columns = pl.ds(pl.multiple_of(at * piece, piece), piece)
        x_grad[:, columns] = row_sum.astype(jnp.bfloat16)
        return 0

    lax.fori_loop(0, pieces, one_sum, 0)

    def finish_owner(target, _):
        pull_copy(target, target, target, target).wait_send()
        back_copy(target, target, target, target).wait_recv()
        return 0

    lax.fori_loop(me + 1, shards, finish_owner, 0)

    def finish_requester(source, _):
        back_copy(source, source, source, source).wait_send()
        ask_copy(source, source, source, source).wait_send()
        return 0

    lax.fori_loop(0, me, finish_requester, 0)


def settle_kernel(blocks, asked, returned, dk, dv, dk_out, dv_out, dk_sum, dv_sum):
    dk_sum[...] = dk[...]
    dv_sum[...] = dv[...]

    def body(target, _):
        for slot in range(CAP):
            unit = asked[target, 0, slot]

            @pl.when(unit >= 0)
            def _():
                rows, cols = unit_place(unit, blocks)
                dk_sum[rows, cols] += returned[target, slot, :, :HD].astype(jnp.float32)
                dv_sum[rows, cols] += returned[target, slot, :, HD:].astype(jnp.float32)

        return 0

    lax.fori_loop(0, returned.shape[0], body, 0)
    dk_out[...] = dk_sum[...].astype(jnp.bfloat16)
    dv_out[...] = dv_sum[...].astype(jnp.bfloat16)


SMEM = pl.BlockSpec(memory_space=pltpu.SMEM)
VMEM = pl.BlockSpec(memory_space=pltpu.VMEM)
LIMIT = pltpu.CompilerParams(vmem_limit_bytes=48 * 2**20)


def per_device(queries, keys, values, outputs, out_grad, log_sum, selected, w_query):
    tokens, width = queries.shape
    heads, blocks, _ = selected.shape
    shards = lax.axis_size("seq")
    me = lax.axis_index("seq")
    unit, mask, local = request_tables(selected, me, shards)
    products = out_grad.astype(jnp.float32) * outputs.astype(jnp.float32)
    delta = jnp.sum(products.reshape(tokens, heads, HD), axis=-1).T
    wide = jax.ShapeDtypeStruct((tokens, width), jnp.float32)
    paired = (shards, CAP, BLOCK, 2 * HD)
    lanes_all = lax.axis_size("head")
    stripe = tokens // lanes_all
    width_in = w_query.shape[0]
    piece = min(512, width_in)
    pieces = width_in // piece
    split = (pieces, lanes_all, stripe, piece)
    x_grad, dk, dv, returned, asked = pl.pallas_call(
        exchange_kernel,
        out_shape=(
            jax.ShapeDtypeStruct((stripe, width_in), jnp.bfloat16),
            wide,
            wide,
            jax.ShapeDtypeStruct(paired, jnp.bfloat16),
            jax.ShapeDtypeStruct((shards, 1, HD), jnp.int32),
        ),
        in_specs=[SMEM] * 3 + [VMEM] * 7 + [pl.BlockSpec(memory_space=pl.ANY)],
        out_specs=(VMEM,) * 5,
        scratch_shapes=[
            pltpu.VMEM(paired, jnp.bfloat16),
            pltpu.VMEM((heads * blocks, BLOCK, 2 * HD), jnp.bfloat16),
            pltpu.SMEM((shards, 1, HD), jnp.int32),
            pltpu.VMEM(paired, jnp.bfloat16),
            pltpu.VMEM(paired, jnp.bfloat16),
            pltpu.VMEM((heads, HD, tokens), jnp.float32),
            pltpu.VMEM((heads, tokens, HD), jnp.bfloat16),
            pltpu.VMEM((heads, tokens, HD), jnp.bfloat16),
            pltpu.VMEM((width_in, width), jnp.bfloat16),
            pltpu.VMEM((tokens, width), jnp.bfloat16),
            pltpu.VMEM(split, jnp.bfloat16),
            pltpu.VMEM(split, jnp.bfloat16),
            pltpu.VMEM(split, jnp.float32),
        ]
        + [pltpu.SemaphoreType.DMA((shards,))] * 4
        + [pltpu.SemaphoreType.DMA((pieces, lanes_all))] * 2
        + [pltpu.SemaphoreType.DMA((shards,))] * 2
        + [pltpu.SemaphoreType.DMA] * 2,
        compiler_params=pltpu.CompilerParams(
            vmem_limit_bytes=56 * 2**20, collective_id=0, has_side_effects=True
        ),
        name="exchange",
    )(
        jnp.maximum(unit.reshape(-1), 0) // blocks,
        mask.reshape(-1),
        local,
        queries,
        keys,
        values,
        out_grad,
        log_sum[:, None, :],
        delta[:, None, :],
        jnp.pad(unit[:, None, :], ((0, 0), (0, 0), (0, HD - CAP)), constant_values=-1),
        w_query,
    )
    result = jax.ShapeDtypeStruct((tokens, width), jnp.bfloat16)
    key_gradient, value_gradient = pl.pallas_call(
        functools.partial(settle_kernel, blocks),
        out_shape=(result, result),
        in_specs=[SMEM] + [VMEM] * 3,
        out_specs=(VMEM, VMEM),
        scratch_shapes=[pltpu.VMEM((tokens, width), jnp.float32)] * 2,
        compiler_params=LIMIT,
        name="settle",
    )(asked, returned, dk, dv)
    return x_grad, key_gradient, value_gradient


def solution(mesh):
    in_specs = (P("seq", "head"),) * 5 + (P("head", "seq"), P("head", "seq", None), P(None, "head"))
    out_specs = (P(("seq", "head"), None), P("seq", "head"), P("seq", "head"))
    return jax.shard_map(
        per_device, mesh=mesh, in_specs=in_specs, out_specs=out_specs, check_vma=False
    )
```

```python
import functools

import jax
import jax.numpy as jnp
from jax import lax
from jax.experimental import pallas as pl
from jax.experimental.pallas import tpu as pltpu
from jax.sharding import PartitionSpec as P

CAP = 2
WINDOW = 12
HD = 128
BLOCK = 64
FAR = 1e30

NT = (((1,), (1,)), ((), ()))
TN = (((0,), (0,)), ((), ()))


def dot(a, b, dims=(((1,), (0,)), ((), ()))):
    return lax.dot_general(a, b, dims, preferred_element_type=jnp.float32)


def smallest(values):
    return jnp.min(functools.reduce(jnp.minimum, values), axis=0, keepdims=True)


def total_of(values):
    return jnp.sum(functools.reduce(jnp.add, values), axis=0, keepdims=True)


def request_tables(selected, me):
    heads, blocks, picks = selected.shape
    units = heads * blocks
    lanes = lax.broadcasted_iota(jnp.int32, (heads, HD), 1)
    head = lax.broadcasted_iota(jnp.int32, (heads, HD), 0)
    bits = [jnp.zeros((heads, HD), jnp.int32) for _ in range(blocks)]
    for query_block in range(blocks):
        rows = selected[:, query_block, :]
        hit = [jnp.zeros((heads, HD), jnp.bool_) for _ in range(blocks)]
        for pick in range(picks):
            entry = jnp.broadcast_to(rows[:, pick : pick + 1], (heads, HD))
            for block in range(blocks):
                hit[block] = hit[block] | (entry == lanes * blocks + block)
        bits = [b + jnp.where(h, 1 << query_block, 0) for b, h in zip(bits, hit)]
    own = jnp.zeros((heads, HD), jnp.int32)
    for block in range(blocks):
        mine = jnp.sum(jnp.where(lanes == me, bits[block], 0), axis=1, keepdims=True)
        own = jnp.where(lanes == block, mine, own)
    bits = [jnp.where(lanes == me, 0, b) for b in bits]
    index = [head * blocks + block for block in range(blocks)]
    first = smallest([jnp.where(b > 0, i, units) for b, i in zip(bits, index)])
    second = smallest([jnp.where((b > 0) & (i > first), i, units) for b, i in zip(bits, index)])
    rows = []
    for at in (first, second):
        rows.append(jnp.where(at == units, -1, at))
    for at in (first, second):
        rows.append(total_of([jnp.where(i == at, b, 0) for b, i in zip(bits, index)]))
    for at in (first, second):
        rows.append(total_of([jnp.where(i == at, head, 0) for i in index]))
    rows += [jnp.zeros_like(first)] * 2
    return jnp.concatenate(rows, axis=0), own


def backward(key, value, query, grad, log_row, delta_row, allowed=None):
    scale = HD**-0.5
    probs = jnp.exp(dot(key, query, NT) * scale - log_row)
    if allowed is not None:
        probs = jnp.where(allowed, probs, 0.0)
    dscores = (probs * (dot(value, grad, NT) - delta_row)).astype(jnp.bfloat16)
    return dot(key, dscores, TN), dot(dscores, query) * scale, dot(probs.astype(jnp.bfloat16), grad)


def offset_of(step, shards):
    return lax.rem(step * 27, shards)


def exchange_kernel(
    selected,
    queries,
    keys,
    values,
    outputs,
    grads,
    log_sum,
    weight,
    x_grad,
    dk,
    dv,
    logs,
    deltas,
    sums_here,
    returned,
    asked,
    outgoing,
    units_here,
    asked_here,
    asking,
    table,
    table_here,
    pulled,
    back,
    total,
    query_heads,
    grad_heads,
    weight_here,
    dq_rows,
    parts_out,
    parts_in,
    own_part,
    pull_send,
    pull_recv,
    back_send,
    back_recv,
    part_send,
    part_recv,
    ask_send,
    ask_recv,
    weight_sem,
    asked_sem,
    table_sem,
):
    me = lax.axis_index("seq")
    lane = lax.axis_index("head")
    shards = asking.shape[0]
    lanes_all = parts_out.shape[1]
    stripe, piece = parts_out.shape[2:]
    pieces = parts_out.shape[0]
    weight_copy = pltpu.make_async_copy(weight, weight_here, weight_sem)
    weight_copy.start()
    asked[...] = jnp.full(asked.shape, -1, jnp.int32)
    requests, own = request_tables(selected, me)
    table[:8] = requests
    table[8:] = own
    table_copy = pltpu.make_async_copy(table, table_here, table_sem)
    table_copy.start()
    turned = jnp.concatenate([requests] + [jnp.zeros((HD - 8, HD), jnp.int32)], axis=0).T
    for source in range(shards):
        asking[source] = turned[source : source + 1, :]
    heads = log_sum.shape[0]
    tokens = queries.shape[0]
    blocks = tokens // BLOCK
    lane_block = lax.broadcasted_iota(jnp.int32, (1, tokens), 1) // BLOCK

    def pull_copy(slot_from, slot_to, target, index):
        return pltpu.make_async_remote_copy(
            src_ref=outgoing.at[slot_from],
            dst_ref=pulled.at[slot_to],
            send_sem=pull_send.at[slot_from],
            recv_sem=pull_recv.at[index],
            device_id={"seq": target},
            device_id_type=pl.DeviceIdType.MESH,
        )

    def back_copy(slot_from, slot_to, target, index):
        return pltpu.make_async_remote_copy(
            src_ref=back.at[slot_from],
            dst_ref=returned.at[slot_to],
            send_sem=back_send.at[slot_from],
            recv_sem=back_recv.at[index],
            device_id={"seq": target},
            device_id_type=pl.DeviceIdType.MESH,
        )

    def ask_copy(slot_from, slot_to, target, index):
        return pltpu.make_async_remote_copy(
            src_ref=asking.at[slot_from],
            dst_ref=asked.at[slot_to],
            send_sem=ask_send.at[slot_from],
            recv_sem=ask_recv.at[index],
            device_id={"seq": target},
            device_id_type=pl.DeviceIdType.MESH,
        )

    def part_copy(at, slot_from, slot_to, target, index):
        return pltpu.make_async_remote_copy(
            src_ref=parts_out.at[at, slot_from],
            dst_ref=parts_in.at[at, slot_to],
            send_sem=part_send.at[at, slot_from],
            recv_sem=part_recv.at[at, index],
            device_id={"head": target},
            device_id_type=pl.DeviceIdType.MESH,
        )

    barrier = pltpu.get_barrier_semaphore()

    def greet(step, _):
        pl.semaphore_signal(
            barrier,
            inc=1,
            device_id={"seq": lax.rem(me + step, shards)},
            device_id_type=pl.DeviceIdType.MESH,
        )
        return 0

    lax.fori_loop(1, shards, greet, 0)
    for step in range(1, lanes_all):
        pl.semaphore_signal(
            barrier,
            inc=1,
            device_id={"head": lax.rem(lane + step, lanes_all)},
            device_id_type=pl.DeviceIdType.MESH,
        )
    pl.semaphore_wait(barrier, shards - 1 + lanes_all - 1)

    def ask(source, _):
        ask_copy(source, me, source, me).start()
        return 0

    lax.fori_loop(0, me, ask, 0)
    for head in range(heads):
        cols = slice(head * HD, (head + 1) * HD)
        query_heads[head] = queries[:, cols]
        grad_heads[head] = grads[:, cols]
        for block in range(blocks):
            rows = slice(block * BLOCK, (block + 1) * BLOCK)
            units_here[head * blocks + block, :, :HD] = keys[rows, cols]
            units_here[head * blocks + block, :, HD:] = values[rows, cols]

    def heard(target, _):
        ask_copy(target, target, target, target).wait_recv()
        return 0

    lax.fori_loop(me + 1, shards, heard, 0)
    asked_copy = pltpu.make_async_copy(asked, asked_here, asked_sem)
    asked_copy.start()
    asked_copy.wait()
    table_copy.wait()

    def send(target):
        for slot in range(CAP):
            wanted = asked_here[target, 0, slot]
            found = units_here[jnp.maximum(wanted, 0)]
            outgoing[target, slot] = jnp.where(
                jnp.full(found.shape, wanted, jnp.int32) >= 0, found, jnp.zeros_like(found)
            )
        pull_copy(target, me, target, me).start()

    def send_step(step, _):
        target = me + offset_of(step, shards)

        @pl.when(target < shards)
        def _():
            send(target)

        return 0

    lax.fori_loop(1, min(WINDOW + 1, shards), send_step, 0)
    for head in range(heads):
        cols = slice(head * HD, (head + 1) * HD)
        products = grads[:, cols].astype(jnp.float32) * outputs[:, cols].astype(jnp.float32)
        deltas[head] = jnp.sum(products.T, axis=0, keepdims=True)
        logs[head] = log_sum[head : head + 1, :]

    def open_logs(head, bits):
        return jnp.where(((bits >> lane_block) & 1) == 1, logs[head], FAR)

    def one_head(head, _):
        cols = pl.ds(pl.multiple_of(head * HD, HD), HD)
        query, grad = query_heads[head], grad_heads[head]
        rows = lax.broadcasted_iota(jnp.int32, (BLOCK, tokens), 0)
        lanes = lax.broadcasted_iota(jnp.int32, (BLOCK, tokens), 1)
        sums = jnp.zeros((HD, tokens), jnp.float32)
        for block in range(blocks):
            place = slice(block * BLOCK, (block + 1) * BLOCK)
            dq, dk_part, dv_part = backward(
                keys[place, cols],
                values[place, cols],
                query,
                grad,
                open_logs(head, table_here[8 + head, block]),
                deltas[head],
                rows + block * BLOCK <= lanes,
            )
            sums += dq
            sums_here[head * blocks + block, :, :HD] = dk_part
            sums_here[head * blocks + block, :, HD:] = dv_part
        total[head] = sums
        return 0

    lax.fori_loop(0, heads, one_head, 0)

    def one_source(step, _):
        source = me - step
        pull_copy(source, source, source, source).wait_recv()
        parts = []
        for slot in range(CAP):
            head = table_here[2 * CAP + slot, source]
            dq, dk_part, dv_part = backward(
                pulled[source, slot, :, :HD],
                pulled[source, slot, :, HD:],
                query_heads[head],
                grad_heads[head],
                open_logs(head, table_here[CAP + slot, source]),
                deltas[head],
            )
            back[source, slot, :, :HD] = dk_part.astype(jnp.bfloat16)
            back[source, slot, :, HD:] = dv_part.astype(jnp.bfloat16)
            parts.append((head, dq))
        back_copy(source, me, source, me).start()
        for head in range(heads):
            total[head] += sum(
                jnp.where(jnp.full(dq.shape, at, jnp.int32) == head, dq, 0.0) for at, dq in parts
            )
        return 0

    def source_step(step, _):
        offset = offset_of(step, shards)

        @pl.when(me + offset < shards)
        def _():
            sent = me + offset
            pull_copy(sent, sent, sent, sent).wait_send()

        @pl.when(step + WINDOW < shards)
        def _():
            send_step(step + WINDOW, 0)

        @pl.when(offset <= me)
        def _():
            one_source(offset, 0)

        return 0

    lax.fori_loop(1, shards, source_step, 0)
    for head in range(heads):
        dq_rows[:, head * HD : (head + 1) * HD] = (total[head] * HD**-0.5).T.astype(jnp.bfloat16)
    weight_copy.wait()

    def one_piece(at, _):
        columns = pl.ds(pl.multiple_of(at * piece, piece), piece)
        product = dot(dq_rows[...], weight_here[columns, :], NT).reshape(lanes_all, stripe, piece)
        own_part[at] = product
        parts_out[at] = product.astype(jnp.bfloat16)
        for step in range(1, lanes_all):
            target = lax.rem(lane + step, lanes_all)
            part_copy(at, target, lane, target, lane).start()
        return 0

    lax.fori_loop(0, pieces, one_piece, 0)

    def one_return(step, _):
        target = me + offset_of(step, shards)

        @pl.when(target < shards)
        def _():
            back_copy(target, target, target, target).wait_recv()
            first, second = (jnp.full((BLOCK, 2 * HD), asked_here[target, 0, i]) for i in range(CAP))

            def one_unit(unit, _):
                late = jnp.where(second == unit, returned[target, 1].astype(jnp.float32), 0.0)
                sums_here[unit] += jnp.where(
                    first == unit, returned[target, 0].astype(jnp.float32), late
                )
                return 0

            lax.fori_loop(0, heads * blocks, one_unit, 0, unroll=4)

        return 0

    lax.fori_loop(1, shards, one_return, 0)
    for head in range(heads):
        cols = slice(head * HD, (head + 1) * HD)
        for block in range(blocks):
            rows = slice(block * BLOCK, (block + 1) * BLOCK)
            both = sums_here[head * blocks + block].astype(jnp.bfloat16)
            dk[rows, cols] = both[:, :HD]
            dv[rows, cols] = both[:, HD:]

    def one_sum(at, _):
        row_sum = own_part[at, lane]
        for step in range(1, lanes_all):
            source = lax.rem(lane + step, lanes_all)
            part_copy(at, source, source, source, source).wait()
            row_sum += parts_in[at, source].astype(jnp.float32)
        columns = pl.ds(pl.multiple_of(at * piece, piece), piece)
        x_grad[:, columns] = row_sum.astype(jnp.bfloat16)
        return 0

    lax.fori_loop(0, pieces, one_sum, 0)

    def finish_requester(source, _):
        back_copy(source, source, source, source).wait_send()
        ask_copy(source, source, source, source).wait_send()
        return 0

    lax.fori_loop(0, me, finish_requester, 0)


VMEM = pl.BlockSpec(memory_space=pltpu.VMEM)


def per_device(queries, keys, values, outputs, out_grad, log_sum, selected, w_query):
    tokens, width = queries.shape
    heads, blocks, _ = selected.shape
    shards = lax.axis_size("seq")
    result = jax.ShapeDtypeStruct((tokens, width), jnp.bfloat16)
    paired = (shards, CAP, BLOCK, 2 * HD)
    lanes_all = lax.axis_size("head")
    stripe = tokens // lanes_all
    width_in = w_query.shape[0]
    piece = min(512, width_in)
    pieces = width_in // piece
    split = (pieces, lanes_all, stripe, piece)
    return pl.pallas_call(
        exchange_kernel,
        out_shape=(
            jax.ShapeDtypeStruct((stripe, width_in), jnp.bfloat16),
            result,
            result,
        ),
        in_specs=[VMEM] * 7 + [pl.BlockSpec(memory_space=pl.ANY)],
        out_specs=(VMEM,) * 3,
        scratch_shapes=[
            pltpu.VMEM((heads, 1, tokens), jnp.float32),
            pltpu.VMEM((heads, 1, tokens), jnp.float32),
            pltpu.VMEM((heads * blocks, BLOCK, 2 * HD), jnp.float32),
            pltpu.VMEM(paired, jnp.bfloat16),
            pltpu.VMEM((shards, 1, HD), jnp.int32),
            pltpu.VMEM(paired, jnp.bfloat16),
            pltpu.VMEM((heads * blocks, BLOCK, 2 * HD), jnp.bfloat16),
            pltpu.SMEM((shards, 1, HD), jnp.int32),
            pltpu.VMEM((shards, 1, HD), jnp.int32),
            pltpu.VMEM((8 + heads, HD), jnp.int32),
            pltpu.SMEM((8 + heads, HD), jnp.int32),
            pltpu.VMEM(paired, jnp.bfloat16),
            pltpu.VMEM(paired, jnp.bfloat16),
            pltpu.VMEM((heads, HD, tokens), jnp.float32),
            pltpu.VMEM((heads, tokens, HD), jnp.bfloat16),
            pltpu.VMEM((heads, tokens, HD), jnp.bfloat16),
            pltpu.VMEM((width_in, width), jnp.bfloat16),
            pltpu.VMEM((tokens, width), jnp.bfloat16),
            pltpu.VMEM(split, jnp.bfloat16),
            pltpu.VMEM(split, jnp.bfloat16),
            pltpu.VMEM(split, jnp.float32),
        ]
        + [pltpu.SemaphoreType.DMA((shards,))] * 4
        + [pltpu.SemaphoreType.DMA((pieces, lanes_all))] * 2
        + [pltpu.SemaphoreType.DMA((shards,))] * 2
        + [pltpu.SemaphoreType.DMA] * 3,
        compiler_params=pltpu.CompilerParams(
            vmem_limit_bytes=56 * 2**20, collective_id=0, has_side_effects=True
        ),
        name="exchange",
    )(
        selected,
        queries,
        keys,
        values,
        outputs,
        out_grad,
        log_sum,
        w_query,
    )


def solution(mesh):
    in_specs = (P("seq", "head"),) * 5 + (P("head", "seq"), P("head", "seq", None), P(None, "head"))
    out_specs = (P(("seq", "head"), None), P("seq", "head"), P("seq", "head"))
    return jax.shard_map(
        per_device, mesh=mesh, in_specs=in_specs, out_specs=out_specs, check_vma=False
    )
```

```python
import functools

import jax
import jax.numpy as jnp
from jax import lax
from jax.experimental import pallas as pl
from jax.experimental.pallas import tpu as pltpu
from jax.sharding import PartitionSpec as P

CAP = 2
WINDOW = 12
LAG = 16
HD = 128
BLOCK = 64
FAR = 1e30

NT = (((1,), (1,)), ((), ()))
TN = (((0,), (0,)), ((), ()))


def dot(a, b, dims=(((1,), (0,)), ((), ()))):
    return lax.dot_general(a, b, dims, preferred_element_type=jnp.float32)


def smallest(values):
    return jnp.min(functools.reduce(jnp.minimum, values), axis=0, keepdims=True)


def total_of(values):
    return jnp.sum(functools.reduce(jnp.add, values), axis=0, keepdims=True)


def request_tables(selected, me):
    heads, blocks, picks = selected.shape
    units = heads * blocks
    lanes = lax.broadcasted_iota(jnp.int32, (heads, HD), 1)
    head = lax.broadcasted_iota(jnp.int32, (heads, HD), 0)
    bits = [jnp.zeros((heads, HD), jnp.int32) for _ in range(blocks)]
    for query_block in range(blocks):
        rows = selected[:, query_block, :]
        hit = [jnp.zeros((heads, HD), jnp.bool_) for _ in range(blocks)]
        for pick in range(picks):
            entry = jnp.broadcast_to(rows[:, pick : pick + 1], (heads, HD))
            for block in range(blocks):
                hit[block] = hit[block] | (entry == lanes * blocks + block)
        bits = [b + jnp.where(h, 1 << query_block, 0) for b, h in zip(bits, hit)]
    own = jnp.zeros((heads, HD), jnp.int32)
    for block in range(blocks):
        mine = jnp.sum(jnp.where(lanes == me, bits[block], 0), axis=1, keepdims=True)
        own = jnp.where(lanes == block, mine, own)
    bits = [jnp.where(lanes == me, 0, b) for b in bits]
    index = [head * blocks + block for block in range(blocks)]
    first = smallest([jnp.where(b > 0, i, units) for b, i in zip(bits, index)])
    second = smallest([jnp.where((b > 0) & (i > first), i, units) for b, i in zip(bits, index)])
    rows = []
    for at in (first, second):
        rows.append(jnp.where(at == units, -1, at))
    for at in (first, second):
        rows.append(total_of([jnp.where(i == at, b, 0) for b, i in zip(bits, index)]))
    for at in (first, second):
        rows.append(total_of([jnp.where(i == at, head, 0) for i in index]))
    rows += [jnp.zeros_like(first)] * 2
    return jnp.concatenate(rows, axis=0), own


def backward(key, value, query, grad, log_row, delta_row, allowed=None):
    scale = HD**-0.5
    probs = jnp.exp(dot(key, query, NT) * scale - log_row)
    if allowed is not None:
        probs = jnp.where(allowed, probs, 0.0)
    dscores = (probs * (dot(value, grad, NT) - delta_row)).astype(jnp.bfloat16)
    return dot(key, dscores, TN), dot(dscores, query) * scale, dot(probs.astype(jnp.bfloat16), grad)


def offset_of(step, shards):
    return lax.rem(step * 27, shards)


def exchange_kernel(
    selected,
    queries,
    keys,
    values,
    outputs,
    grads,
    log_sum,
    weight,
    x_grad,
    dk,
    dv,
    logs,
    deltas,
    sums_here,
    returned,
    asked,
    outgoing,
    units_here,
    asked_here,
    asking,
    table,
    table_here,
    pulled,
    back,
    total,
    query_heads,
    grad_heads,
    weight_here,
    dq_rows,
    parts_out,
    parts_in,
    relay_in,
    own_part,
    pull_send,
    pull_recv,
    back_send,
    back_recv,
    part_send,
    part_recv,
    relay_recv,
    ask_send,
    ask_recv,
    weight_sem,
    asked_sem,
    table_sem,
):
    me = lax.axis_index("seq")
    lane = lax.axis_index("head")
    shards = asking.shape[0]
    lanes_all = parts_out.shape[1]
    up, far, down = (lax.rem(lane + step, lanes_all) for step in (1, 2, 3))
    stripe, piece = parts_out.shape[2:]
    pieces = parts_out.shape[0]
    asked[...] = jnp.full(asked.shape, -1, jnp.int32)
    heads = log_sum.shape[0]
    tokens = queries.shape[0]
    blocks = tokens // BLOCK
    lane_block = lax.broadcasted_iota(jnp.int32, (1, tokens), 1) // BLOCK

    def pull_copy(slot_from, slot_to, target, index):
        return pltpu.make_async_remote_copy(
            src_ref=outgoing.at[slot_from],
            dst_ref=pulled.at[slot_to],
            send_sem=pull_send.at[slot_from],
            recv_sem=pull_recv.at[index],
            device_id={"seq": target},
            device_id_type=pl.DeviceIdType.MESH,
        )

    def back_copy(slot_from, slot_to, target, index):
        return pltpu.make_async_remote_copy(
            src_ref=back.at[slot_from],
            dst_ref=returned.at[slot_to],
            send_sem=back_send.at[slot_from],
            recv_sem=back_recv.at[index],
            device_id={"seq": target},
            device_id_type=pl.DeviceIdType.MESH,
        )

    def ask_copy(slot_from, slot_to, target, index):
        return pltpu.make_async_remote_copy(
            src_ref=asking.at[slot_from],
            dst_ref=asked.at[slot_to],
            send_sem=ask_send.at[slot_from],
            recv_sem=ask_recv.at[index],
            device_id={"seq": target},
            device_id_type=pl.DeviceIdType.MESH,
        )

    def relay_copy(at, slot, target):
        return pltpu.make_async_remote_copy(
            src_ref=parts_out.at[at, slot],
            dst_ref=relay_in.at[at],
            send_sem=part_send.at[at, slot],
            recv_sem=relay_recv.at[at],
            device_id={"head": target},
            device_id_type=pl.DeviceIdType.MESH,
        )

    def part_copy(at, target, side):
        return pltpu.make_async_remote_copy(
            src_ref=parts_out.at[at, target],
            dst_ref=parts_in.at[at, side],
            send_sem=part_send.at[at, target],
            recv_sem=part_recv.at[at, side],
            device_id={"head": target},
            device_id_type=pl.DeviceIdType.MESH,
        )

    barrier = pltpu.get_barrier_semaphore()

    def greet(step, _):
        pl.semaphore_signal(
            barrier,
            inc=1,
            device_id={"seq": lax.rem(me + step, shards)},
            device_id_type=pl.DeviceIdType.MESH,
        )
        return 0

    lax.fori_loop(1, shards, greet, 0)
    for neighbour in (up, down):
        pl.semaphore_signal(
            barrier,
            inc=1,
            device_id={"head": neighbour},
            device_id_type=pl.DeviceIdType.MESH,
        )
    weight_copy = pltpu.make_async_copy(weight, weight_here, weight_sem)
    weight_copy.start()
    requests, own = request_tables(selected, me)
    table[:8] = requests
    table[8:] = own
    table_copy = pltpu.make_async_copy(table, table_here, table_sem)
    table_copy.start()
    turned = jnp.concatenate([requests] + [jnp.zeros((HD - 8, HD), jnp.int32)], axis=0).T
    for source in range(shards):
        asking[source] = turned[source : source + 1, :]
    pl.semaphore_wait(barrier, shards - 1 + 2)

    def ask(source, _):
        ask_copy(source, me, source, me).start()
        return 0

    lax.fori_loop(0, me, ask, 0)
    for head in range(heads):
        cols = slice(head * HD, (head + 1) * HD)
        query_heads[head] = queries[:, cols]
        grad_heads[head] = grads[:, cols]
        for block in range(blocks):
            rows = slice(block * BLOCK, (block + 1) * BLOCK)
            units_here[head * blocks + block, :, :HD] = keys[rows, cols]
            units_here[head * blocks + block, :, HD:] = values[rows, cols]

    def heard(target, _):
        ask_copy(target, target, target, target).wait_recv()
        return 0

    lax.fori_loop(me + 1, shards, heard, 0)
    asked_copy = pltpu.make_async_copy(asked, asked_here, asked_sem)
    asked_copy.start()
    asked_copy.wait()
    table_copy.wait()

    def send(target):
        for slot in range(CAP):
            wanted = asked_here[target, 0, slot]
            found = units_here[jnp.maximum(wanted, 0)]
            outgoing[target, slot] = jnp.where(
                jnp.full(found.shape, wanted, jnp.int32) >= 0, found, jnp.zeros_like(found)
            )
        pull_copy(target, me, target, me).start()

    def send_step(step, _):
        target = me + offset_of(step, shards)

        @pl.when(target < shards)
        def _():
            send(target)

        return 0

    lax.fori_loop(1, min(WINDOW + 1, shards), send_step, 0)
    for head in range(heads):
        cols = slice(head * HD, (head + 1) * HD)
        products = grads[:, cols].astype(jnp.float32) * outputs[:, cols].astype(jnp.float32)
        deltas[head] = jnp.sum(products.T, axis=0, keepdims=True)
        logs[head] = log_sum[head : head + 1, :]

    def open_logs(head, bits):
        return jnp.where(((bits >> lane_block) & 1) == 1, logs[head], FAR)

    def one_head(head, _):
        cols = pl.ds(pl.multiple_of(head * HD, HD), HD)
        query, grad = query_heads[head], grad_heads[head]
        rows = lax.broadcasted_iota(jnp.int32, (BLOCK, tokens), 0)
        lanes = lax.broadcasted_iota(jnp.int32, (BLOCK, tokens), 1)
        sums = jnp.zeros((HD, tokens), jnp.float32)
        for block in range(blocks):
            place = slice(block * BLOCK, (block + 1) * BLOCK)
            dq, dk_part, dv_part = backward(
                keys[place, cols],
                values[place, cols],
                query,
                grad,
                open_logs(head, table_here[8 + head, block]),
                deltas[head],
                rows + block * BLOCK <= lanes,
            )
            sums += dq
            sums_here[head * blocks + block, :, :HD] = dk_part
            sums_here[head * blocks + block, :, HD:] = dv_part
        total[head] = sums
        return 0

    lax.fori_loop(0, heads, one_head, 0)

    def one_source(step, _):
        source = me - step
        pull_copy(source, source, source, source).wait_recv()
        parts = []
        for slot in range(CAP):
            head = table_here[2 * CAP + slot, source]
            dq, dk_part, dv_part = backward(
                pulled[source, slot, :, :HD],
                pulled[source, slot, :, HD:],
                query_heads[head],
                grad_heads[head],
                open_logs(head, table_here[CAP + slot, source]),
                deltas[head],
            )
            back[source, slot, :, :HD] = dk_part.astype(jnp.bfloat16)
            back[source, slot, :, HD:] = dv_part.astype(jnp.bfloat16)
            parts.append((head, dq))
        back_copy(source, me, source, me).start()
        for head in range(heads):
            total[head] += sum(
                jnp.where(jnp.full(dq.shape, at, jnp.int32) == head, dq, 0.0) for at, dq in parts
            )
        return 0

    def one_return(step, _):
        target = me + offset_of(step, shards)

        @pl.when(target < shards)
        def _():
            back_copy(target, target, target, target).wait_recv()
            first, second = (jnp.full((BLOCK, 2 * HD), asked_here[target, 0, i]) for i in range(CAP))

            def one_unit(unit, _):
                late = jnp.where(second == unit, returned[target, 1].astype(jnp.float32), 0.0)
                sums_here[unit] += jnp.where(
                    first == unit, returned[target, 0].astype(jnp.float32), late
                )
                return 0

            lax.fori_loop(0, heads * blocks, one_unit, 0, unroll=4)

        return 0

    def source_step(step, _):
        offset = offset_of(step, shards)

        @pl.when(me + offset < shards)
        def _():
            sent = me + offset
            pull_copy(sent, sent, sent, sent).wait_send()

        @pl.when(step + WINDOW < shards)
        def _():
            send_step(step + WINDOW, 0)

        @pl.when(offset <= me)
        def _():
            one_source(offset, 0)

        @pl.when(step > LAG)
        def _():
            one_return(step - LAG, 0)

        return 0

    lax.fori_loop(1, shards, source_step, 0)
    for head in range(heads):
        dq_rows[:, head * HD : (head + 1) * HD] = (total[head] * HD**-0.5).T.astype(jnp.bfloat16)
    weight_copy.wait()

    half = pieces // 2

    def one_piece(at, toward):
        columns = pl.ds(pl.multiple_of(at * piece, piece), piece)
        product = dot(dq_rows[...], weight_here[columns, :], NT).reshape(lanes_all, stripe, piece)
        own_part[at] = product
        parts_out[at] = product.astype(jnp.bfloat16)
        relay_copy(at, far, toward).start()

    def two_pieces(at, _):
        one_piece(at, up)
        one_piece(half + at, down)
        return 0

    lax.fori_loop(0, half, two_pieces, 0)

    def two_direct(at, _):
        part_copy(at, down, 1).start()
        part_copy(half + at, up, 0).start()
        return 0

    lax.fori_loop(0, half, two_direct, 0)

    def one_relay(at, target, origin, side):
        relay_copy(at, far, origin).wait_recv()
        joined = own_part[at, target] + relay_in[at].astype(jnp.float32)
        parts_out[at, target] = joined.astype(jnp.bfloat16)
        part_copy(at, target, side).start()

    def two_relays(at, _):
        one_relay(at, up, down, 0)
        one_relay(half + at, down, up, 1)
        return 0

    lax.fori_loop(0, half, two_relays, 0)

    lax.fori_loop(max(1, shards - LAG), shards, one_return, 0)
    for head in range(heads):
        cols = slice(head * HD, (head + 1) * HD)
        for block in range(blocks):
            rows = slice(block * BLOCK, (block + 1) * BLOCK)
            both = sums_here[head * blocks + block].astype(jnp.bfloat16)
            dk[rows, cols] = both[:, :HD]
            dv[rows, cols] = both[:, HD:]

    def one_sum(at, _):
        row_sum = own_part[at, lane]
        for side, target in ((0, up), (1, down)):
            part_copy(at, target, side).wait()
            row_sum += parts_in[at, side].astype(jnp.float32)
        relay_copy(at, far, up).wait_send()
        columns = pl.ds(pl.multiple_of(at * piece, piece), piece)
        x_grad[:, columns] = row_sum.astype(jnp.bfloat16)
        return 0

    lax.fori_loop(0, pieces, one_sum, 0)

    def finish_requester(source, _):
        back_copy(source, source, source, source).wait_send()
        ask_copy(source, source, source, source).wait_send()
        return 0

    lax.fori_loop(0, me, finish_requester, 0)


def hand_out_kernel(*refs):
    for given, result in zip(refs[:3], refs[3:]):
        result[...] = given[...]


VMEM = pl.BlockSpec(memory_space=pltpu.VMEM)


def per_device(queries, keys, values, outputs, out_grad, log_sum, selected, w_query):
    tokens, width = queries.shape
    heads, blocks, _ = selected.shape
    shards = lax.axis_size("seq")
    result = jax.ShapeDtypeStruct((tokens, width), jnp.bfloat16)
    paired = (shards, CAP, BLOCK, 2 * HD)
    lanes_all = lax.axis_size("head")
    stripe = tokens // lanes_all
    width_in = w_query.shape[0]
    piece = min(512, width_in // 2)
    pieces = width_in // piece
    split = (pieces, lanes_all, stripe, piece)
    arrays = pl.pallas_call(
        exchange_kernel,
        out_shape=(
            jax.ShapeDtypeStruct((stripe, width_in), jnp.bfloat16),
            result,
            result,
        ),
        in_specs=[VMEM] * 7 + [pl.BlockSpec(memory_space=pl.ANY)],
        out_specs=(VMEM,) * 3,
        scratch_shapes=[
            pltpu.VMEM((heads, 1, tokens), jnp.float32),
            pltpu.VMEM((heads, 1, tokens), jnp.float32),
            pltpu.VMEM((heads * blocks, BLOCK, 2 * HD), jnp.float32),
            pltpu.VMEM(paired, jnp.bfloat16),
            pltpu.VMEM((shards, 1, HD), jnp.int32),
            pltpu.VMEM(paired, jnp.bfloat16),
            pltpu.VMEM((heads * blocks, BLOCK, 2 * HD), jnp.bfloat16),
            pltpu.SMEM((shards, 1, HD), jnp.int32),
            pltpu.VMEM((shards, 1, HD), jnp.int32),
            pltpu.VMEM((8 + heads, HD), jnp.int32),
            pltpu.SMEM((8 + heads, HD), jnp.int32),
            pltpu.VMEM(paired, jnp.bfloat16),
            pltpu.VMEM(paired, jnp.bfloat16),
            pltpu.VMEM((heads, HD, tokens), jnp.float32),
            pltpu.VMEM((heads, tokens, HD), jnp.bfloat16),
            pltpu.VMEM((heads, tokens, HD), jnp.bfloat16),
            pltpu.VMEM((width_in, width), jnp.bfloat16),
            pltpu.VMEM((tokens, width), jnp.bfloat16),
            pltpu.VMEM(split, jnp.bfloat16),
            pltpu.VMEM((pieces, 2, stripe, piece), jnp.bfloat16),
            pltpu.VMEM((pieces, stripe, piece), jnp.bfloat16),
            pltpu.VMEM(split, jnp.float32),
        ]
        + [pltpu.SemaphoreType.DMA((shards,))] * 4
        + [pltpu.SemaphoreType.DMA((pieces, lanes_all)), pltpu.SemaphoreType.DMA((pieces, 2))]
        + [pltpu.SemaphoreType.DMA((pieces,))]
        + [pltpu.SemaphoreType.DMA((shards,))] * 2
        + [pltpu.SemaphoreType.DMA] * 3,
        compiler_params=pltpu.CompilerParams(
            vmem_limit_bytes=56 * 2**20, collective_id=0, has_side_effects=True
        ),
        name="exchange",
    )(
        selected,
        queries,
        keys,
        values,
        outputs,
        out_grad,
        log_sum,
        w_query,
    )
    return pl.pallas_call(
        hand_out_kernel,
        out_shape=tuple(jax.ShapeDtypeStruct(a.shape, a.dtype) for a in arrays),
        in_specs=[VMEM] * 3,
        out_specs=(VMEM,) * 3,
        name="hand_out",
    )(*arrays)


def solution(mesh):
    in_specs = (P("seq", "head"),) * 5 + (P("head", "seq"), P("head", "seq", None), P(None, "head"))
    out_specs = (P(("seq", "head"), None), P("seq", "head"), P("seq", "head"))
    return jax.shard_map(
        per_device, mesh=mesh, in_specs=in_specs, out_specs=out_specs, check_vma=False
    )
```

```python
import functools

import jax
import jax.numpy as jnp
from jax import lax
from jax.experimental import pallas as pl
from jax.experimental.pallas import tpu as pltpu
from jax.sharding import PartitionSpec as P

CAP = 2
WINDOW = 14
LAG = 20
HD = 128
BLOCK = 64
FAR = 1e30

NT = (((1,), (1,)), ((), ()))
TN = (((0,), (0,)), ((), ()))


def dot(a, b, dims=(((1,), (0,)), ((), ()))):
    return lax.dot_general(a, b, dims, preferred_element_type=jnp.float32)


def smallest(values):
    return jnp.min(functools.reduce(jnp.minimum, values), axis=0, keepdims=True)


def total_of(values):
    return jnp.sum(functools.reduce(jnp.add, values), axis=0, keepdims=True)


def request_tables(selected, me):
    heads, blocks, picks = selected.shape
    units = heads * blocks
    lanes = lax.broadcasted_iota(jnp.int32, (heads, HD), 1)
    head = lax.broadcasted_iota(jnp.int32, (heads, HD), 0)
    bits = [jnp.zeros((heads, HD), jnp.int32) for _ in range(blocks)]
    for query_block in range(blocks):
        rows = selected[:, query_block, :]
        hit = [jnp.zeros((heads, HD), jnp.bool_) for _ in range(blocks)]
        for pick in range(picks):
            entry = jnp.broadcast_to(rows[:, pick : pick + 1], (heads, HD))
            for block in range(blocks):
                hit[block] = hit[block] | (entry == lanes * blocks + block)
        bits = [b + jnp.where(h, 1 << query_block, 0) for b, h in zip(bits, hit)]
    own = jnp.zeros((heads, HD), jnp.int32)
    for block in range(blocks):
        mine = jnp.sum(jnp.where(lanes == me, bits[block], 0), axis=1, keepdims=True)
        own = jnp.where(lanes == block, mine, own)
    bits = [jnp.where(lanes == me, 0, b) for b in bits]
    index = [head * blocks + block for block in range(blocks)]
    first = smallest([jnp.where(b > 0, i, units) for b, i in zip(bits, index)])
    second = smallest([jnp.where((b > 0) & (i > first), i, units) for b, i in zip(bits, index)])
    rows = []
    for at in (first, second):
        rows.append(jnp.where(at == units, -1, at))
    for at in (first, second):
        rows.append(total_of([jnp.where(i == at, b, 0) for b, i in zip(bits, index)]))
    for at in (first, second):
        rows.append(total_of([jnp.where(i == at, head, 0) for i in index]))
    rows += [jnp.zeros_like(first)] * 2
    return jnp.concatenate(rows, axis=0), own


def backward(key, value, query, grad, log_row, delta_row, allowed=None):
    scale = HD**-0.5
    probs = jnp.exp(dot(key, query, NT) * scale - log_row)
    if allowed is not None:
        probs = jnp.where(allowed, probs, 0.0)
    dscores = (probs * (dot(value, grad, NT) - delta_row)).astype(jnp.bfloat16)
    return dot(key, dscores, TN), dot(dscores, query) * scale, dot(probs.astype(jnp.bfloat16), grad)


def offset_of(step, shards):
    return lax.rem(step * 27, shards)


def exchange_kernel(
    selected,
    queries_far,
    keys_far,
    values_far,
    outputs_far,
    grads_far,
    log_sum,
    weight,
    x_grad,
    dk,
    dv,
    queries,
    keys,
    values,
    outputs,
    grads,
    logs,
    deltas,
    sums_here,
    returned,
    asked,
    asked_late,
    outgoing,
    units_here,
    asked_here,
    asked_late_here,
    asking,
    table,
    table_here,
    pulled,
    back,
    total,
    query_heads,
    grad_heads,
    weight_here,
    dq_rows,
    parts_out,
    parts_in,
    relay_in,
    own_part,
    pull_send,
    pull_recv,
    back_send,
    back_recv,
    part_send,
    part_recv,
    relay_recv,
    ask_send,
    ask_recv,
    weight_sem,
    asked_sem,
    table_sem,
    load_sem,
    late_sem,
):
    me = lax.axis_index("seq")
    lane = lax.axis_index("head")
    shards = asking.shape[0]
    lanes_all = parts_out.shape[1]
    up, far, down = (lax.rem(lane + step, lanes_all) for step in (1, 2, 3))
    stripe, piece = parts_out.shape[2:]
    pieces = parts_out.shape[0]
    asked[...] = jnp.full(asked.shape, -1, jnp.int32)
    asked_late[...] = jnp.full(asked.shape, -1, jnp.int32)
    far_refs = (keys_far, values_far, queries_far, grads_far, outputs_far)
    near_refs = (keys, values, queries, grads, outputs)
    loads = [
        pltpu.make_async_copy(*pair, load_sem.at[i]) for i, pair in enumerate(zip(far_refs, near_refs))
    ]
    heads = log_sum.shape[0]
    tokens = queries.shape[0]
    blocks = tokens // BLOCK
    lane_block = lax.broadcasted_iota(jnp.int32, (1, tokens), 1) // BLOCK

    def pull_copy(slot_from, slot_to, target, index):
        return pltpu.make_async_remote_copy(
            src_ref=outgoing.at[slot_from],
            dst_ref=pulled.at[slot_to],
            send_sem=pull_send.at[slot_from],
            recv_sem=pull_recv.at[index],
            device_id={"seq": target},
            device_id_type=pl.DeviceIdType.MESH,
        )

    def back_copy(slot_from, slot_to, target, index):
        return pltpu.make_async_remote_copy(
            src_ref=back.at[slot_from],
            dst_ref=returned.at[slot_to],
            send_sem=back_send.at[slot_from],
            recv_sem=back_recv.at[index],
            device_id={"seq": target},
            device_id_type=pl.DeviceIdType.MESH,
        )

    early = min(WINDOW + 1, shards)

    def ask_copy(landing, slot_from, slot_to, target, index):
        return pltpu.make_async_remote_copy(
            src_ref=asking.at[slot_from],
            dst_ref=landing.at[slot_to],
            send_sem=ask_send.at[slot_from],
            recv_sem=ask_recv.at[index],
            device_id={"seq": target},
            device_id_type=pl.DeviceIdType.MESH,
        )

    def relay_copy(at, slot, target):
        return pltpu.make_async_remote_copy(
            src_ref=parts_out.at[at, slot],
            dst_ref=relay_in.at[at],
            send_sem=part_send.at[at, slot],
            recv_sem=relay_recv.at[at],
            device_id={"head": target},
            device_id_type=pl.DeviceIdType.MESH,
        )

    def part_copy(at, target, side):
        return pltpu.make_async_remote_copy(
            src_ref=parts_out.at[at, target],
            dst_ref=parts_in.at[at, side],
            send_sem=part_send.at[at, target],
            recv_sem=part_recv.at[at, side],
            device_id={"head": target},
            device_id_type=pl.DeviceIdType.MESH,
        )

    barrier = pltpu.get_barrier_semaphore()

    def greet(step, _):
        pl.semaphore_signal(
            barrier,
            inc=1,
            device_id={"seq": lax.rem(me + step, shards)},
            device_id_type=pl.DeviceIdType.MESH,
        )
        return 0

    lax.fori_loop(1, shards, greet, 0)
    for neighbour in (up, down):
        pl.semaphore_signal(
            barrier,
            inc=1,
            device_id={"head": neighbour},
            device_id_type=pl.DeviceIdType.MESH,
        )
    for load in loads:
        load.start()
    weight_copy = pltpu.make_async_copy(weight, weight_here, weight_sem)
    weight_copy.start()
    requests, own = request_tables(selected, me)
    table[:8] = requests
    table[8:] = own
    table_copy = pltpu.make_async_copy(table, table_here, table_sem)
    table_copy.start()
    turned = jnp.concatenate([requests] + [jnp.zeros((HD - 8, HD), jnp.int32)], axis=0).T
    for source in range(shards):
        asking[source] = turned[source : source + 1, :]
    pl.semaphore_wait(barrier, shards - 1 + 2)

    def ask(landing, step, _):
        source = me - offset_of(step, shards)

        @pl.when(source >= 0)
        def _():
            ask_copy(landing, source, me, source, me).start()

        return 0

    def heard(landing, step, _):
        target = me + offset_of(step, shards)

        @pl.when(target < shards)
        def _():
            ask_copy(landing, target, target, target, target).wait_recv()

        return 0

    def send_step(wanted_here, step, _):
        target = me + offset_of(step, shards)

        @pl.when(target < shards)
        def _():
            for slot in range(CAP):
                wanted = wanted_here[target, 0, slot]
                found = units_here[jnp.maximum(wanted, 0)]
                outgoing[target, slot] = jnp.where(
                    jnp.full(found.shape, wanted, jnp.int32) >= 0, found, jnp.zeros_like(found)
                )
            pull_copy(target, me, target, me).start()

        return 0

    lax.fori_loop(1, early, functools.partial(ask, asked), 0)
    for load in loads[:2]:
        load.wait()
    for head in range(heads):
        cols = slice(head * HD, (head + 1) * HD)
        for block in range(blocks):
            rows = slice(block * BLOCK, (block + 1) * BLOCK)
            units_here[head * blocks + block, :, :HD] = keys[rows, cols]
            units_here[head * blocks + block, :, HD:] = values[rows, cols]
    lax.fori_loop(1, early, functools.partial(heard, asked), 0)
    asked_copy = pltpu.make_async_copy(asked, asked_here, asked_sem)
    asked_copy.start()
    asked_copy.wait()
    lax.fori_loop(1, early, functools.partial(send_step, asked_here), 0)
    lax.fori_loop(early, shards, functools.partial(ask, asked_late), 0)
    for load in loads[2:]:
        load.wait()
    for head in range(heads):
        cols = slice(head * HD, (head + 1) * HD)
        query_heads[head] = queries[:, cols]
        grad_heads[head] = grads[:, cols]
    table_copy.wait()
    lax.fori_loop(early, shards, functools.partial(heard, asked_late), 0)
    late_copy = pltpu.make_async_copy(asked_late, asked_late_here, late_sem)
    late_copy.start()
    late_copy.wait()
    for head in range(heads):
        cols = slice(head * HD, (head + 1) * HD)
        products = grads[:, cols].astype(jnp.float32) * outputs[:, cols].astype(jnp.float32)
        deltas[head] = jnp.sum(products.T, axis=0, keepdims=True)
        logs[head] = log_sum[head : head + 1, :]

    def open_logs(head, bits):
        return jnp.where(((bits >> lane_block) & 1) == 1, logs[head], FAR)

    def one_head(head, _):
        cols = pl.ds(pl.multiple_of(head * HD, HD), HD)
        query, grad = query_heads[head], grad_heads[head]
        rows = lax.broadcasted_iota(jnp.int32, (BLOCK, tokens), 0)
        lanes = lax.broadcasted_iota(jnp.int32, (BLOCK, tokens), 1)
        sums = jnp.zeros((HD, tokens), jnp.float32)
        for block in range(blocks):
            place = slice(block * BLOCK, (block + 1) * BLOCK)
            dq, dk_part, dv_part = backward(
                keys[place, cols],
                values[place, cols],
                query,
                grad,
                open_logs(head, table_here[8 + head, block]),
                deltas[head],
                rows + block * BLOCK <= lanes,
            )
            sums += dq
            sums_here[head * blocks + block, :, :HD] = dk_part
            sums_here[head * blocks + block, :, HD:] = dv_part
        total[head] = sums
        return 0

    lax.fori_loop(0, heads, one_head, 0)

    def one_source(step, _):
        source = me - step
        pull_copy(source, source, source, source).wait_recv()
        parts = []
        for slot in range(CAP):
            head = table_here[2 * CAP + slot, source]
            dq, dk_part, dv_part = backward(
                pulled[source, slot, :, :HD],
                pulled[source, slot, :, HD:],
                query_heads[head],
                grad_heads[head],
                open_logs(head, table_here[CAP + slot, source]),
                deltas[head],
            )
            back[source, slot, :, :HD] = dk_part.astype(jnp.bfloat16)
            back[source, slot, :, HD:] = dv_part.astype(jnp.bfloat16)
            parts.append((head, dq))
        back_copy(source, me, source, me).start()
        for head in range(heads):
            total[head] += sum(
                jnp.where(jnp.full(dq.shape, at, jnp.int32) == head, dq, 0.0) for at, dq in parts
            )
        return 0

    def one_return(step, _):
        target = me + offset_of(step, shards)

        @pl.when(target < shards)
        def _():
            back_copy(target, target, target, target).wait_recv()
            first, second = (
                jnp.full(
                    (BLOCK, 2 * HD),
                    jnp.where(step < early, asked_here[target, 0, i], asked_late_here[target, 0, i]),
                )
                for i in range(CAP)
            )

            def one_unit(unit, _):
                late = jnp.where(second == unit, returned[target, 1].astype(jnp.float32), 0.0)
                sums_here[unit] += jnp.where(
                    first == unit, returned[target, 0].astype(jnp.float32), late
                )
                return 0

            lax.fori_loop(0, heads * blocks, one_unit, 0, unroll=4)

        return 0

    def source_step(step, _):
        offset = offset_of(step, shards)

        @pl.when(me + offset < shards)
        def _():
            sent = me + offset
            pull_copy(sent, sent, sent, sent).wait_send()

        @pl.when(step + WINDOW < shards)
        def _():
            send_step(asked_late_here, step + WINDOW, 0)

        @pl.when(offset <= me)
        def _():
            one_source(offset, 0)

        @pl.when(step > LAG)
        def _():
            one_return(step - LAG, 0)

        return 0

    lax.fori_loop(1, shards, source_step, 0)
    for head in range(heads):
        dq_rows[:, head * HD : (head + 1) * HD] = (total[head] * HD**-0.5).T.astype(jnp.bfloat16)
    weight_copy.wait()

    half = pieces // 2

    def one_piece(at, toward):
        columns = pl.ds(pl.multiple_of(at * piece, piece), piece)
        product = dot(dq_rows[...], weight_here[columns, :], NT).reshape(lanes_all, stripe, piece)
        own_part[at] = product
        parts_out[at] = product.astype(jnp.bfloat16)
        relay_copy(at, far, toward).start()

    def two_pieces(at, _):
        one_piece(at, up)
        one_piece(half + at, down)
        return 0

    lax.fori_loop(0, half, two_pieces, 0)

    def two_direct(at, _):
        part_copy(at, down, 1).start()
        part_copy(half + at, up, 0).start()
        return 0

    lax.fori_loop(0, half, two_direct, 0)

    def one_relay(at, target, origin, side):
        relay_copy(at, far, origin).wait_recv()
        joined = own_part[at, target] + relay_in[at].astype(jnp.float32)
        parts_out[at, target] = joined.astype(jnp.bfloat16)
        part_copy(at, target, side).start()

    def two_relays(at, _):
        one_relay(at, up, down, 0)
        one_relay(half + at, down, up, 1)
        return 0

    lax.fori_loop(0, half, two_relays, 0)

    lax.fori_loop(max(1, shards - LAG), shards, one_return, 0)
    for head in range(heads):
        cols = slice(head * HD, (head + 1) * HD)
        for block in range(blocks):
            rows = slice(block * BLOCK, (block + 1) * BLOCK)
            both = sums_here[head * blocks + block].astype(jnp.bfloat16)
            dk[rows, cols] = both[:, :HD]
            dv[rows, cols] = both[:, HD:]

    def one_sum(at, _):
        row_sum = own_part[at, lane]
        for side, target in ((0, up), (1, down)):
            part_copy(at, target, side).wait()
            row_sum += parts_in[at, side].astype(jnp.float32)
        relay_copy(at, far, up).wait_send()
        columns = pl.ds(pl.multiple_of(at * piece, piece), piece)
        x_grad[:, columns] = row_sum.astype(jnp.bfloat16)
        return 0

    lax.fori_loop(0, pieces, one_sum, 0)

    def finish_requester(source, _):
        back_copy(source, source, source, source).wait_send()
        ask_copy(asked, source, source, source, source).wait_send()
        return 0

    lax.fori_loop(0, me, finish_requester, 0)


def hand_out_kernel(*refs):
    for given, result in zip(refs[:3], refs[3:]):
        result[...] = given[...]


HELD = pl.BlockSpec(memory_space=pl.ANY)
VMEM = pl.BlockSpec(memory_space=pltpu.VMEM)


def per_device(queries, keys, values, outputs, out_grad, log_sum, selected, w_query):
    tokens, width = queries.shape
    heads, blocks, _ = selected.shape
    shards = lax.axis_size("seq")
    result = jax.ShapeDtypeStruct((tokens, width), jnp.bfloat16)
    paired = (shards, CAP, BLOCK, 2 * HD)
    lanes_all = lax.axis_size("head")
    stripe = tokens // lanes_all
    width_in = w_query.shape[0]
    piece = min(512, width_in // 2)
    pieces = width_in // piece
    split = (pieces, lanes_all, stripe, piece)
    arrays = pl.pallas_call(
        exchange_kernel,
        out_shape=(
            jax.ShapeDtypeStruct((stripe, width_in), jnp.bfloat16),
            result,
            result,
        ),
        in_specs=[VMEM] + [HELD] * 5 + [VMEM, HELD],
        out_specs=(VMEM,) * 3,
        scratch_shapes=[pltpu.VMEM((tokens, width), jnp.bfloat16)] * 5
        + [
            pltpu.VMEM((heads, 1, tokens), jnp.float32),
            pltpu.VMEM((heads, 1, tokens), jnp.float32),
            pltpu.VMEM((heads * blocks, BLOCK, 2 * HD), jnp.float32),
            pltpu.VMEM(paired, jnp.bfloat16),
            pltpu.VMEM((shards, 1, HD), jnp.int32),
            pltpu.VMEM((shards, 1, HD), jnp.int32),
            pltpu.VMEM(paired, jnp.bfloat16),
            pltpu.VMEM((heads * blocks, BLOCK, 2 * HD), jnp.bfloat16),
            pltpu.SMEM((shards, 1, HD), jnp.int32),
            pltpu.SMEM((shards, 1, HD), jnp.int32),
            pltpu.VMEM((shards, 1, HD), jnp.int32),
            pltpu.VMEM((8 + heads, HD), jnp.int32),
            pltpu.SMEM((8 + heads, HD), jnp.int32),
            pltpu.VMEM(paired, jnp.bfloat16),
            pltpu.VMEM(paired, jnp.bfloat16),
            pltpu.VMEM((heads, HD, tokens), jnp.float32),
            pltpu.VMEM((heads, tokens, HD), jnp.bfloat16),
            pltpu.VMEM((heads, tokens, HD), jnp.bfloat16),
            pltpu.VMEM((width_in, width), jnp.bfloat16),
            pltpu.VMEM((tokens, width), jnp.bfloat16),
            pltpu.VMEM(split, jnp.bfloat16),
            pltpu.VMEM((pieces, 2, stripe, piece), jnp.bfloat16),
            pltpu.VMEM((pieces, stripe, piece), jnp.bfloat16),
            pltpu.VMEM(split, jnp.float32),
        ]
        + [pltpu.SemaphoreType.DMA((shards,))] * 4
        + [pltpu.SemaphoreType.DMA((pieces, lanes_all)), pltpu.SemaphoreType.DMA((pieces, 2))]
        + [pltpu.SemaphoreType.DMA((pieces,))]
        + [pltpu.SemaphoreType.DMA((shards,))] * 2
        + [pltpu.SemaphoreType.DMA] * 3
        + [pltpu.SemaphoreType.DMA((5,)), pltpu.SemaphoreType.DMA],
        compiler_params=pltpu.CompilerParams(
            vmem_limit_bytes=56 * 2**20, collective_id=0, has_side_effects=True
        ),
        name="exchange",
    )(
        selected,
        queries,
        keys,
        values,
        outputs,
        out_grad,
        log_sum,
        w_query,
    )
    return pl.pallas_call(
        hand_out_kernel,
        out_shape=tuple(jax.ShapeDtypeStruct(a.shape, a.dtype) for a in arrays),
        in_specs=[VMEM] * 3,
        out_specs=(VMEM,) * 3,
        name="hand_out",
    )(*arrays)


def solution(mesh):
    in_specs = (P("seq", "head"),) * 5 + (P("head", "seq"), P("head", "seq", None), P(None, "head"))
    out_specs = (P(("seq", "head"), None), P("seq", "head"), P("seq", "head"))
    return jax.shard_map(
        per_device, mesh=mesh, in_specs=in_specs, out_specs=out_specs, check_vma=False
    )
```

```python
import functools

import jax
import jax.numpy as jnp
from jax import lax
from jax.experimental import pallas as pl
from jax.experimental.pallas import tpu as pltpu
from jax.sharding import PartitionSpec as P

CAP = 2
WINDOW = 14
LAG = 20
HD = 128
BLOCK = 64
FAR = 1e30

NT = (((1,), (1,)), ((), ()))
TN = (((0,), (0,)), ((), ()))


def dot(a, b, dims=(((1,), (0,)), ((), ()))):
    return lax.dot_general(a, b, dims, preferred_element_type=jnp.float32)


def smallest(values):
    return jnp.min(functools.reduce(jnp.minimum, values), axis=0, keepdims=True)


def total_of(values):
    return jnp.sum(functools.reduce(jnp.add, values), axis=0, keepdims=True)


def request_tables(selected, me):
    heads, blocks, picks = selected.shape
    units = heads * blocks
    lanes = lax.broadcasted_iota(jnp.int32, (heads, HD), 1)
    head = lax.broadcasted_iota(jnp.int32, (heads, HD), 0)
    bits = [jnp.zeros((heads, HD), jnp.int32) for _ in range(blocks)]
    for query_block in range(blocks):
        rows = selected[:, query_block, :]
        hit = [jnp.zeros((heads, HD), jnp.bool_) for _ in range(blocks)]
        for pick in range(picks):
            entry = jnp.broadcast_to(rows[:, pick : pick + 1], (heads, HD))
            for block in range(blocks):
                hit[block] = hit[block] | (entry == lanes * blocks + block)
        bits = [b + jnp.where(h, 1 << query_block, 0) for b, h in zip(bits, hit)]
    own = jnp.zeros((heads, HD), jnp.int32)
    for block in range(blocks):
        mine = jnp.sum(jnp.where(lanes == me, bits[block], 0), axis=1, keepdims=True)
        own = jnp.where(lanes == block, mine, own)
    bits = [jnp.where(lanes == me, 0, b) for b in bits]
    index = [head * blocks + block for block in range(blocks)]
    first = smallest([jnp.where(b > 0, i, units) for b, i in zip(bits, index)])
    second = smallest([jnp.where((b > 0) & (i > first), i, units) for b, i in zip(bits, index)])
    rows = []
    for at in (first, second):
        rows.append(jnp.where(at == units, -1, at))
    for at in (first, second):
        rows.append(total_of([jnp.where(i == at, b, 0) for b, i in zip(bits, index)]))
    for at in (first, second):
        rows.append(total_of([jnp.where(i == at, head, 0) for i in index]))
    rows += [jnp.zeros_like(first)] * 2
    return jnp.concatenate(rows, axis=0), own


def backward(key, value, query, grad, log_row, delta_row, allowed=None):
    scale = HD**-0.5
    probs = jnp.exp(dot(key, query, NT) * scale - log_row)
    if allowed is not None:
        probs = jnp.where(allowed, probs, 0.0)
    dscores = (probs * (dot(value, grad, NT) - delta_row)).astype(jnp.bfloat16)
    return dot(key, dscores, TN), dot(dscores, query) * scale, dot(probs.astype(jnp.bfloat16), grad)


def offset_of(step, shards):
    return lax.rem(step * 27, shards)


def exchange_kernel(
    selected,
    queries_far,
    keys_far,
    values_far,
    outputs_far,
    grads_far,
    log_sum,
    weight,
    x_grad,
    dk,
    dv,
    queries,
    keys,
    values,
    outputs,
    grads,
    logs,
    deltas,
    sums_here,
    returned,
    asked,
    asked_late,
    outgoing,
    units_here,
    asked_here,
    asked_late_here,
    asking,
    table,
    table_here,
    pulled,
    back,
    total,
    query_heads,
    grad_heads,
    weight_here,
    dq_rows,
    parts_out,
    parts_in,
    relay_in,
    own_part,
    pull_send,
    pull_recv,
    back_send,
    back_recv,
    part_send,
    part_recv,
    relay_recv,
    ask_send,
    ask_recv,
    weight_sem,
    asked_sem,
    table_sem,
    load_sem,
    late_sem,
):
    me = lax.axis_index("seq")
    lane = lax.axis_index("head")
    shards = asking.shape[0]
    lanes_all = parts_out.shape[1]
    up, far, down = (lax.rem(lane + step, lanes_all) for step in (1, 2, 3))
    stripe, piece = parts_out.shape[2:]
    pieces = parts_out.shape[0]
    asked[...] = jnp.full(asked.shape, -1, jnp.int32)
    asked_late[...] = jnp.full(asked.shape, -1, jnp.int32)
    far_refs = (keys_far, values_far, queries_far, grads_far, outputs_far)
    near_refs = (keys, values, queries, grads, outputs)
    loads = [
        pltpu.make_async_copy(*pair, load_sem.at[i]) for i, pair in enumerate(zip(far_refs, near_refs))
    ]
    heads = log_sum.shape[0]
    tokens = queries.shape[0]
    blocks = tokens // BLOCK
    lane_block = lax.broadcasted_iota(jnp.int32, (1, tokens), 1) // BLOCK

    def pull_copy(slot_from, slot_to, target, index):
        return pltpu.make_async_remote_copy(
            src_ref=outgoing.at[slot_from],
            dst_ref=pulled.at[slot_to],
            send_sem=pull_send.at[slot_from],
            recv_sem=pull_recv.at[index],
            device_id={"seq": target},
            device_id_type=pl.DeviceIdType.MESH,
        )

    def back_copy(slot_from, slot_to, target, index):
        return pltpu.make_async_remote_copy(
            src_ref=back.at[slot_from],
            dst_ref=returned.at[slot_to],
            send_sem=back_send.at[slot_from],
            recv_sem=back_recv.at[index],
            device_id={"seq": target},
            device_id_type=pl.DeviceIdType.MESH,
        )

    early = min(WINDOW + 1, shards)

    def ask_copy(landing, slot_from, slot_to, target, index):
        return pltpu.make_async_remote_copy(
            src_ref=asking.at[slot_from],
            dst_ref=landing.at[slot_to],
            send_sem=ask_send.at[slot_from],
            recv_sem=ask_recv.at[index],
            device_id={"seq": target},
            device_id_type=pl.DeviceIdType.MESH,
        )

    def relay_copy(at, slot, target):
        return pltpu.make_async_remote_copy(
            src_ref=parts_out.at[at, slot],
            dst_ref=relay_in.at[at],
            send_sem=part_send.at[at, slot],
            recv_sem=relay_recv.at[at],
            device_id={"head": target},
            device_id_type=pl.DeviceIdType.MESH,
        )

    def part_copy(at, target, side):
        return pltpu.make_async_remote_copy(
            src_ref=parts_out.at[at, target],
            dst_ref=parts_in.at[at, side],
            send_sem=part_send.at[at, target],
            recv_sem=part_recv.at[at, side],
            device_id={"head": target},
            device_id_type=pl.DeviceIdType.MESH,
        )

    barrier = pltpu.get_barrier_semaphore()

    def greet(step, _):
        pl.semaphore_signal(
            barrier,
            inc=1,
            device_id={"seq": lax.rem(me + step, shards)},
            device_id_type=pl.DeviceIdType.MESH,
        )
        return 0

    lax.fori_loop(1, shards, greet, 0)
    for neighbour in (up, down):
        pl.semaphore_signal(
            barrier,
            inc=1,
            device_id={"head": neighbour},
            device_id_type=pl.DeviceIdType.MESH,
        )
    for load in loads:
        load.start()
    weight_copy = pltpu.make_async_copy(weight, weight_here, weight_sem)
    weight_copy.start()
    requests, own = request_tables(selected, me)
    table[:8] = requests
    table[8:] = own
    table_copy = pltpu.make_async_copy(table, table_here, table_sem)
    table_copy.start()
    turned = jnp.concatenate([requests] + [jnp.zeros((HD - 8, HD), jnp.int32)], axis=0).T
    for source in range(shards):
        asking[source] = turned[source : source + 1, :]
    pl.semaphore_wait(barrier, shards - 1 + 2)

    def ask(landing, step, _):
        source = me - offset_of(step, shards)

        @pl.when(source >= 0)
        def _():
            ask_copy(landing, source, me, source, me).start()

        return 0

    def heard(landing, step, _):
        target = me + offset_of(step, shards)

        @pl.when(target < shards)
        def _():
            ask_copy(landing, target, target, target, target).wait_recv()

        return 0

    def send_step(wanted_here, step, _):
        target = me + offset_of(step, shards)

        @pl.when(target < shards)
        def _():
            for slot in range(CAP):
                wanted = wanted_here[target, 0, slot]
                found = units_here[jnp.maximum(wanted, 0)]
                outgoing[target, slot] = jnp.where(
                    jnp.full(found.shape, wanted, jnp.int32) >= 0, found, jnp.zeros_like(found)
                )
            pull_copy(target, me, target, me).start()

        return 0

    lax.fori_loop(1, early, functools.partial(ask, asked), 0)
    for load in loads[:2]:
        load.wait()
    for head in range(heads):
        cols = slice(head * HD, (head + 1) * HD)
        for block in range(blocks):
            rows = slice(block * BLOCK, (block + 1) * BLOCK)
            units_here[head * blocks + block, :, :HD] = keys[rows, cols]
            units_here[head * blocks + block, :, HD:] = values[rows, cols]
    lax.fori_loop(1, early, functools.partial(heard, asked), 0)
    asked_copy = pltpu.make_async_copy(asked, asked_here, asked_sem)
    asked_copy.start()
    asked_copy.wait()
    lax.fori_loop(1, early, functools.partial(send_step, asked_here), 0)
    lax.fori_loop(early, shards, functools.partial(ask, asked_late), 0)
    for load in loads[2:]:
        load.wait()
    for head in range(heads):
        cols = slice(head * HD, (head + 1) * HD)
        query_heads[head] = queries[:, cols]
        grad_heads[head] = grads[:, cols]
    table_copy.wait()
    lax.fori_loop(early, shards, functools.partial(heard, asked_late), 0)
    late_copy = pltpu.make_async_copy(asked_late, asked_late_here, late_sem)
    late_copy.start()
    late_copy.wait()
    for head in range(heads):
        cols = slice(head * HD, (head + 1) * HD)
        products = grads[:, cols].astype(jnp.float32) * outputs[:, cols].astype(jnp.float32)
        deltas[head] = jnp.sum(products.T, axis=0, keepdims=True)
        logs[head] = log_sum[head : head + 1, :]

    def open_logs(head, bits):
        return jnp.where(((bits >> lane_block) & 1) == 1, logs[head], FAR)

    def one_head(head, _):
        cols = pl.ds(pl.multiple_of(head * HD, HD), HD)
        query, grad = query_heads[head], grad_heads[head]
        rows = lax.broadcasted_iota(jnp.int32, (BLOCK, tokens), 0)
        lanes = lax.broadcasted_iota(jnp.int32, (BLOCK, tokens), 1)
        sums = jnp.zeros((HD, tokens), jnp.float32)
        for block in range(blocks):
            place = slice(block * BLOCK, (block + 1) * BLOCK)
            dq, dk_part, dv_part = backward(
                keys[place, cols],
                values[place, cols],
                query,
                grad,
                open_logs(head, table_here[8 + head, block]),
                deltas[head],
                rows + block * BLOCK <= lanes,
            )
            sums += dq
            sums_here[head * blocks + block, :, :HD] = dk_part
            sums_here[head * blocks + block, :, HD:] = dv_part
        total[head] = sums
        return 0

    lax.fori_loop(0, heads, one_head, 0)

    def one_source(step, _):
        source = me - step
        pull_copy(source, source, source, source).wait_recv()
        parts = []
        for slot in range(CAP):
            head = table_here[2 * CAP + slot, source]
            dq, dk_part, dv_part = backward(
                pulled[source, slot, :, :HD],
                pulled[source, slot, :, HD:],
                query_heads[head],
                grad_heads[head],
                open_logs(head, table_here[CAP + slot, source]),
                deltas[head],
            )
            back[source, slot, :, :HD] = dk_part.astype(jnp.bfloat16)
            back[source, slot, :, HD:] = dv_part.astype(jnp.bfloat16)
            parts.append((head, dq))
        back_copy(source, me, source, me).start()
        for head in range(heads):
            total[head] += sum(
                jnp.where(jnp.full(dq.shape, at, jnp.int32) == head, dq, 0.0) for at, dq in parts
            )
        return 0

    def one_return(step, _):
        target = me + offset_of(step, shards)

        @pl.when(target < shards)
        def _():
            back_copy(target, target, target, target).wait_recv()
            first, second = (
                jnp.full(
                    (BLOCK, 2 * HD),
                    jnp.where(step < early, asked_here[target, 0, i], asked_late_here[target, 0, i]),
                )
                for i in range(CAP)
            )

            def one_unit(unit, _):
                late = jnp.where(second == unit, returned[target, 1].astype(jnp.float32), 0.0)
                sums_here[unit] += jnp.where(
                    first == unit, returned[target, 0].astype(jnp.float32), late
                )
                return 0

            lax.fori_loop(0, heads * blocks, one_unit, 0, unroll=4)

        return 0

    def sent_step(step, _):
        sent = me + offset_of(step, shards)

        @pl.when(sent < shards)
        def _():
            pull_copy(sent, sent, sent, sent).wait_send()

        return 0

    def source_step(step, _):
        offset = offset_of(step, shards)

        @pl.when(step + WINDOW < shards)
        def _():
            sent_step(step, 0)
            send_step(asked_late_here, step + WINDOW, 0)

        @pl.when(offset <= me)
        def _():
            one_source(offset, 0)

        @pl.when(step > LAG)
        def _():
            one_return(step - LAG, 0)

        return 0

    lax.fori_loop(1, shards, source_step, 0)
    for head in range(heads):
        dq_rows[:, head * HD : (head + 1) * HD] = (total[head] * HD**-0.5).T.astype(jnp.bfloat16)
    weight_copy.wait()

    half = pieces // 2

    def one_piece(at, toward):
        columns = pl.ds(pl.multiple_of(at * piece, piece), piece)
        product = dot(dq_rows[...], weight_here[columns, :], NT).reshape(lanes_all, stripe, piece)
        own_part[at] = product
        parts_out[at] = product.astype(jnp.bfloat16)
        relay_copy(at, far, toward).start()

    def two_pieces(at, _):
        one_piece(at, up)
        one_piece(half + at, down)
        return 0

    lax.fori_loop(0, half, two_pieces, 0)

    def two_direct(at, _):
        part_copy(at, down, 1).start()
        part_copy(half + at, up, 0).start()
        return 0

    lax.fori_loop(0, half, two_direct, 0)

    def one_relay(at, target, origin, side):
        relay_copy(at, far, origin).wait_recv()
        joined = own_part[at, target] + relay_in[at].astype(jnp.float32)
        parts_out[at, target] = joined.astype(jnp.bfloat16)
        part_copy(at, target, side).start()

    def two_relays(at, _):
        one_relay(at, up, down, 0)
        one_relay(half + at, down, up, 1)
        return 0

    lax.fori_loop(0, half, two_relays, 0)

    lax.fori_loop(max(1, shards - LAG), shards, one_return, 0)
    for head in range(heads):
        cols = slice(head * HD, (head + 1) * HD)
        for block in range(blocks):
            rows = slice(block * BLOCK, (block + 1) * BLOCK)
            both = sums_here[head * blocks + block].astype(jnp.bfloat16)
            dk[rows, cols] = both[:, :HD]
            dv[rows, cols] = both[:, HD:]

    def one_sum(at, _):
        row_sum = own_part[at, lane]
        for side, target in ((0, up), (1, down)):
            part_copy(at, target, side).wait()
            row_sum += parts_in[at, side].astype(jnp.float32)
        relay_copy(at, far, up).wait_send()
        columns = pl.ds(pl.multiple_of(at * piece, piece), piece)
        x_grad[:, columns] = row_sum.astype(jnp.bfloat16)
        return 0

    lax.fori_loop(0, pieces, one_sum, 0)

    lax.fori_loop(max(1, shards - WINDOW), shards, sent_step, 0)

    def finish_requester(source, _):
        back_copy(source, source, source, source).wait_send()
        ask_copy(asked, source, source, source, source).wait_send()
        return 0

    lax.fori_loop(0, me, finish_requester, 0)


def hand_out_kernel(*refs):
    for given, result in zip(refs[:3], refs[3:]):
        result[...] = given[...]


HELD = pl.BlockSpec(memory_space=pl.ANY)
VMEM = pl.BlockSpec(memory_space=pltpu.VMEM)


def per_device(queries, keys, values, outputs, out_grad, log_sum, selected, w_query):
    tokens, width = queries.shape
    heads, blocks, _ = selected.shape
    shards = lax.axis_size("seq")
    result = jax.ShapeDtypeStruct((tokens, width), jnp.bfloat16)
    paired = (shards, CAP, BLOCK, 2 * HD)
    lanes_all = lax.axis_size("head")
    stripe = tokens // lanes_all
    width_in = w_query.shape[0]
    piece = min(512, width_in // 2)
    pieces = width_in // piece
    split = (pieces, lanes_all, stripe, piece)
    arrays = pl.pallas_call(
        exchange_kernel,
        out_shape=(
            jax.ShapeDtypeStruct((stripe, width_in), jnp.bfloat16),
            result,
            result,
        ),
        in_specs=[VMEM] + [HELD] * 5 + [VMEM, HELD],
        out_specs=(VMEM,) * 3,
        scratch_shapes=[pltpu.VMEM((tokens, width), jnp.bfloat16)] * 5
        + [
            pltpu.VMEM((heads, 1, tokens), jnp.float32),
            pltpu.VMEM((heads, 1, tokens), jnp.float32),
            pltpu.VMEM((heads * blocks, BLOCK, 2 * HD), jnp.float32),
            pltpu.VMEM(paired, jnp.bfloat16),
            pltpu.VMEM((shards, 1, HD), jnp.int32),
            pltpu.VMEM((shards, 1, HD), jnp.int32),
            pltpu.VMEM(paired, jnp.bfloat16),
            pltpu.VMEM((heads * blocks, BLOCK, 2 * HD), jnp.bfloat16),
            pltpu.SMEM((shards, 1, HD), jnp.int32),
            pltpu.SMEM((shards, 1, HD), jnp.int32),
            pltpu.VMEM((shards, 1, HD), jnp.int32),
            pltpu.VMEM((8 + heads, HD), jnp.int32),
            pltpu.SMEM((8 + heads, HD), jnp.int32),
            pltpu.VMEM(paired, jnp.bfloat16),
            pltpu.VMEM(paired, jnp.bfloat16),
            pltpu.VMEM((heads, HD, tokens), jnp.float32),
            pltpu.VMEM((heads, tokens, HD), jnp.bfloat16),
            pltpu.VMEM((heads, tokens, HD), jnp.bfloat16),
            pltpu.VMEM((width_in, width), jnp.bfloat16),
            pltpu.VMEM((tokens, width), jnp.bfloat16),
            pltpu.VMEM(split, jnp.bfloat16),
            pltpu.VMEM((pieces, 2, stripe, piece), jnp.bfloat16),
            pltpu.VMEM((pieces, stripe, piece), jnp.bfloat16),
            pltpu.VMEM(split, jnp.float32),
        ]
        + [pltpu.SemaphoreType.DMA((shards,))] * 4
        + [pltpu.SemaphoreType.DMA((pieces, lanes_all)), pltpu.SemaphoreType.DMA((pieces, 2))]
        + [pltpu.SemaphoreType.DMA((pieces,))]
        + [pltpu.SemaphoreType.DMA((shards,))] * 2
        + [pltpu.SemaphoreType.DMA] * 3
        + [pltpu.SemaphoreType.DMA((5,)), pltpu.SemaphoreType.DMA],
        compiler_params=pltpu.CompilerParams(
            vmem_limit_bytes=56 * 2**20, collective_id=0, has_side_effects=True
        ),
        name="exchange",
    )(
        selected,
        queries,
        keys,
        values,
        outputs,
        out_grad,
        log_sum,
        w_query,
    )
    return pl.pallas_call(
        hand_out_kernel,
        out_shape=tuple(jax.ShapeDtypeStruct(a.shape, a.dtype) for a in arrays),
        in_specs=[VMEM] * 3,
        out_specs=(VMEM,) * 3,
        name="hand_out",
    )(*arrays)


def solution(mesh):
    in_specs = (P("seq", "head"),) * 5 + (P("head", "seq"), P("head", "seq", None), P(None, "head"))
    out_specs = (P(("seq", "head"), None), P("seq", "head"), P("seq", "head"))
    return jax.shard_map(
        per_device, mesh=mesh, in_specs=in_specs, out_specs=out_specs, check_vma=False
    )
```

```python
import functools

import jax
import jax.numpy as jnp
from jax import lax
from jax.experimental import pallas as pl
from jax.experimental.pallas import tpu as pltpu
from jax.sharding import PartitionSpec as P

CAP = 2
WINDOW = 14
LAG = 20
HD = 128
BLOCK = 64
FAR = 1e30

NT = (((1,), (1,)), ((), ()))
TN = (((0,), (0,)), ((), ()))


def dot(a, b, dims=(((1,), (0,)), ((), ()))):
    return lax.dot_general(a, b, dims, preferred_element_type=jnp.float32)


def smallest(values):
    return jnp.min(functools.reduce(jnp.minimum, values), axis=0, keepdims=True)


def total_of(values):
    return jnp.sum(functools.reduce(jnp.add, values), axis=0, keepdims=True)


def request_tables(selected, me):
    heads, blocks, picks = selected.shape
    units = heads * blocks
    lanes = lax.broadcasted_iota(jnp.int32, (heads, HD), 1)
    head = lax.broadcasted_iota(jnp.int32, (heads, HD), 0)
    bits = [jnp.zeros((heads, HD), jnp.int32) for _ in range(blocks)]
    for query_block in range(blocks):
        rows = selected[:, query_block, :]
        hit = [jnp.zeros((heads, HD), jnp.bool_) for _ in range(blocks)]
        for pick in range(picks):
            entry = jnp.broadcast_to(rows[:, pick : pick + 1], (heads, HD))
            for block in range(blocks):
                hit[block] = hit[block] | (entry == lanes * blocks + block)
        bits = [b + jnp.where(h, 1 << query_block, 0) for b, h in zip(bits, hit)]
    own = jnp.zeros((heads, HD), jnp.int32)
    for block in range(blocks):
        mine = jnp.sum(jnp.where(lanes == me, bits[block], 0), axis=1, keepdims=True)
        own = jnp.where(lanes == block, mine, own)
    bits = [jnp.where(lanes == me, 0, b) for b in bits]
    index = [head * blocks + block for block in range(blocks)]
    first = smallest([jnp.where(b > 0, i, units) for b, i in zip(bits, index)])
    second = smallest([jnp.where((b > 0) & (i > first), i, units) for b, i in zip(bits, index)])
    rows = []
    for at in (first, second):
        rows.append(jnp.where(at == units, -1, at))
    for at in (first, second):
        rows.append(total_of([jnp.where(i == at, b, 0) for b, i in zip(bits, index)]))
    for at in (first, second):
        rows.append(total_of([jnp.where(i == at, head, 0) for i in index]))
    rows += [jnp.zeros_like(first)] * 2
    return jnp.concatenate(rows, axis=0), own


def backward(key, value, query, grad, log_row, delta_row, allowed=None):
    scale = HD**-0.5
    probs = jnp.exp(dot(key, query, NT) * scale - log_row)
    if allowed is not None:
        probs = jnp.where(allowed, probs, 0.0)
    dscores = (probs * (dot(value, grad, NT) - delta_row)).astype(jnp.bfloat16)
    return dot(key, dscores, TN), dot(dscores, query) * scale, dot(probs.astype(jnp.bfloat16), grad)


def offset_of(step, shards):
    return lax.rem(step * 19, shards)


def exchange_kernel(
    selected,
    queries_far,
    keys_far,
    values_far,
    outputs_far,
    grads_far,
    log_sum,
    weight,
    x_grad,
    dk,
    dv,
    queries,
    keys,
    values,
    outputs,
    grads,
    logs,
    deltas,
    sums_here,
    returned,
    asked,
    asked_late,
    outgoing,
    units_here,
    asked_here,
    asked_late_here,
    asking,
    table,
    table_here,
    pulled,
    back,
    total,
    query_heads,
    grad_heads,
    weight_here,
    dq_rows,
    parts_out,
    parts_in,
    relay_in,
    own_part,
    pull_send,
    pull_recv,
    back_send,
    back_recv,
    part_send,
    part_recv,
    relay_recv,
    ask_send,
    ask_recv,
    weight_sem,
    asked_sem,
    table_sem,
    load_sem,
    late_sem,
):
    me = lax.axis_index("seq")
    lane = lax.axis_index("head")
    shards = asking.shape[0]
    lanes_all = parts_out.shape[1]
    up, far, down = (lax.rem(lane + step, lanes_all) for step in (1, 2, 3))
    stripe, piece = parts_out.shape[2:]
    pieces = parts_out.shape[0]
    asked[...] = jnp.full(asked.shape, -1, jnp.int32)
    asked_late[...] = jnp.full(asked.shape, -1, jnp.int32)
    far_refs = (keys_far, values_far, queries_far, grads_far, outputs_far)
    near_refs = (keys, values, queries, grads, outputs)
    loads = [
        pltpu.make_async_copy(*pair, load_sem.at[i]) for i, pair in enumerate(zip(far_refs, near_refs))
    ]
    heads = log_sum.shape[0]
    tokens = queries.shape[0]
    blocks = tokens // BLOCK
    lane_block = lax.broadcasted_iota(jnp.int32, (1, tokens), 1) // BLOCK

    def pull_copy(slot_from, slot_to, target, index):
        return pltpu.make_async_remote_copy(
            src_ref=outgoing.at[slot_from],
            dst_ref=pulled.at[slot_to],
            send_sem=pull_send.at[slot_from],
            recv_sem=pull_recv.at[index],
            device_id={"seq": target},
            device_id_type=pl.DeviceIdType.MESH,
        )

    def back_copy(slot_from, slot_to, target, index):
        return pltpu.make_async_remote_copy(
            src_ref=back.at[slot_from],
            dst_ref=returned.at[slot_to],
            send_sem=back_send.at[slot_from],
            recv_sem=back_recv.at[index],
            device_id={"seq": target},
            device_id_type=pl.DeviceIdType.MESH,
        )

    early = min(WINDOW + 1, shards)

    def ask_copy(landing, slot_from, slot_to, target, index):
        return pltpu.make_async_remote_copy(
            src_ref=asking.at[slot_from],
            dst_ref=landing.at[slot_to],
            send_sem=ask_send.at[slot_from],
            recv_sem=ask_recv.at[index],
            device_id={"seq": target},
            device_id_type=pl.DeviceIdType.MESH,
        )

    def relay_copy(at, slot, target):
        return pltpu.make_async_remote_copy(
            src_ref=parts_out.at[at, slot],
            dst_ref=relay_in.at[at],
            send_sem=part_send.at[at, slot],
            recv_sem=relay_recv.at[at],
            device_id={"head": target},
            device_id_type=pl.DeviceIdType.MESH,
        )

    def part_copy(at, target, side):
        return pltpu.make_async_remote_copy(
            src_ref=parts_out.at[at, target],
            dst_ref=parts_in.at[at, side],
            send_sem=part_send.at[at, target],
            recv_sem=part_recv.at[at, side],
            device_id={"head": target},
            device_id_type=pl.DeviceIdType.MESH,
        )

    barrier = pltpu.get_barrier_semaphore()

    def greet(step, _):
        pl.semaphore_signal(
            barrier,
            inc=1,
            device_id={"seq": lax.rem(me + step, shards)},
            device_id_type=pl.DeviceIdType.MESH,
        )
        return 0

    lax.fori_loop(1, shards, greet, 0)
    for neighbour in (up, down):
        pl.semaphore_signal(
            barrier,
            inc=1,
            device_id={"head": neighbour},
            device_id_type=pl.DeviceIdType.MESH,
        )
    for load in loads:
        load.start()
    weight_copy = pltpu.make_async_copy(weight, weight_here, weight_sem)
    weight_copy.start()
    requests, own = request_tables(selected, me)
    table[:8] = requests
    table[8:] = own
    table_copy = pltpu.make_async_copy(table, table_here, table_sem)
    table_copy.start()
    turned = jnp.concatenate([requests] + [jnp.zeros((HD - 8, HD), jnp.int32)], axis=0).T
    for source in range(shards):
        asking[source] = turned[source : source + 1, :]
    pl.semaphore_wait(barrier, shards - 1 + 2)

    def ask(landing, step, _):
        source = me - offset_of(step, shards)

        @pl.when(source >= 0)
        def _():
            ask_copy(landing, source, me, source, me).start()

        return 0

    def heard(landing, step, _):
        target = me + offset_of(step, shards)

        @pl.when(target < shards)
        def _():
            ask_copy(landing, target, target, target, target).wait_recv()

        return 0

    def send_step(wanted_here, step, _):
        target = me + offset_of(step, shards)

        @pl.when(target < shards)
        def _():
            for slot in range(CAP):
                wanted = wanted_here[target, 0, slot]
                found = units_here[jnp.maximum(wanted, 0)]
                outgoing[target, slot] = jnp.where(
                    jnp.full(found.shape, wanted, jnp.int32) >= 0, found, jnp.zeros_like(found)
                )
            pull_copy(target, me, target, me).start()

        return 0

    lax.fori_loop(1, early, functools.partial(ask, asked), 0)
    for load in loads[:2]:
        load.wait()
    for head in range(heads):
        cols = slice(head * HD, (head + 1) * HD)
        for block in range(blocks):
            rows = slice(block * BLOCK, (block + 1) * BLOCK)
            units_here[head * blocks + block, :, :HD] = keys[rows, cols]
            units_here[head * blocks + block, :, HD:] = values[rows, cols]
    lax.fori_loop(1, early, functools.partial(heard, asked), 0)
    asked_copy = pltpu.make_async_copy(asked, asked_here, asked_sem)
    asked_copy.start()
    asked_copy.wait()
    lax.fori_loop(1, early, functools.partial(send_step, asked_here), 0)
    lax.fori_loop(early, shards, functools.partial(ask, asked_late), 0)
    for load in loads[2:]:
        load.wait()
    for head in range(heads):
        cols = slice(head * HD, (head + 1) * HD)
        query_heads[head] = queries[:, cols]
        grad_heads[head] = grads[:, cols]
    table_copy.wait()
    lax.fori_loop(early, shards, functools.partial(heard, asked_late), 0)
    late_copy = pltpu.make_async_copy(asked_late, asked_late_here, late_sem)
    late_copy.start()
    late_copy.wait()
    for head in range(heads):
        cols = slice(head * HD, (head + 1) * HD)
        products = grads[:, cols].astype(jnp.float32) * outputs[:, cols].astype(jnp.float32)
        deltas[head] = jnp.sum(products.T, axis=0, keepdims=True)
        logs[head] = log_sum[head : head + 1, :]

    def open_logs(head, bits):
        return jnp.where(((bits >> lane_block) & 1) == 1, logs[head], FAR)

    def one_head(head, _):
        cols = pl.ds(pl.multiple_of(head * HD, HD), HD)
        query, grad = query_heads[head], grad_heads[head]
        rows = lax.broadcasted_iota(jnp.int32, (BLOCK, tokens), 0)
        lanes = lax.broadcasted_iota(jnp.int32, (BLOCK, tokens), 1)
        sums = jnp.zeros((HD, tokens), jnp.float32)
        for block in range(blocks):
            place = slice(block * BLOCK, (block + 1) * BLOCK)
            dq, dk_part, dv_part = backward(
                keys[place, cols],
                values[place, cols],
                query,
                grad,
                open_logs(head, table_here[8 + head, block]),
                deltas[head],
                rows + block * BLOCK <= lanes,
            )
            sums += dq
            sums_here[head * blocks + block, :, :HD] = dk_part
            sums_here[head * blocks + block, :, HD:] = dv_part
        total[head] = sums
        return 0

    lax.fori_loop(0, heads, one_head, 0)

    def one_source(step, _):
        source = me - step
        pull_copy(source, source, source, source).wait_recv()
        parts = []
        for slot in range(CAP):
            head = table_here[2 * CAP + slot, source]
            dq, dk_part, dv_part = backward(
                pulled[source, slot, :, :HD],
                pulled[source, slot, :, HD:],
                query_heads[head],
                grad_heads[head],
                open_logs(head, table_here[CAP + slot, source]),
                deltas[head],
            )
            back[source, slot, :, :HD] = dk_part.astype(jnp.bfloat16)
            back[source, slot, :, HD:] = dv_part.astype(jnp.bfloat16)
            parts.append((head, dq))
        back_copy(source, me, source, me).start()
        for head in range(heads):
            total[head] += sum(
                jnp.where(jnp.full(dq.shape, at, jnp.int32) == head, dq, 0.0) for at, dq in parts
            )
        return 0

    def one_return(step, _):
        target = me + offset_of(step, shards)

        @pl.when(target < shards)
        def _():
            back_copy(target, target, target, target).wait_recv()
            first, second = (
                jnp.full(
                    (BLOCK, 2 * HD),
                    jnp.where(step < early, asked_here[target, 0, i], asked_late_here[target, 0, i]),
                )
                for i in range(CAP)
            )

            def one_unit(unit, _):
                late = jnp.where(second == unit, returned[target, 1].astype(jnp.float32), 0.0)
                sums_here[unit] += jnp.where(
                    first == unit, returned[target, 0].astype(jnp.float32), late
                )
                return 0

            lax.fori_loop(0, heads * blocks, one_unit, 0, unroll=4)

        return 0

    def sent_step(step, _):
        sent = me + offset_of(step, shards)

        @pl.when(sent < shards)
        def _():
            pull_copy(sent, sent, sent, sent).wait_send()

        return 0

    def source_step(step, _):
        offset = offset_of(step, shards)

        @pl.when(step + WINDOW < shards)
        def _():
            sent_step(step, 0)
            send_step(asked_late_here, step + WINDOW, 0)

        @pl.when(offset <= me)
        def _():
            one_source(offset, 0)

        @pl.when(step > LAG)
        def _():
            one_return(step - LAG, 0)

        return 0

    lax.fori_loop(1, shards, source_step, 0)
    for head in range(heads):
        dq_rows[:, head * HD : (head + 1) * HD] = (total[head] * HD**-0.5).T.astype(jnp.bfloat16)
    weight_copy.wait()

    half = pieces // 2

    def one_piece(at, toward):
        columns = pl.ds(pl.multiple_of(at * piece, piece), piece)
        product = dot(dq_rows[...], weight_here[columns, :], NT).reshape(lanes_all, stripe, piece)
        own_part[at] = product
        parts_out[at] = product.astype(jnp.bfloat16)
        relay_copy(at, far, toward).start()

    def two_pieces(at, _):
        one_piece(at, up)
        one_piece(half + at, down)
        return 0

    lax.fori_loop(0, half, two_pieces, 0)

    def two_direct(at, _):
        part_copy(at, down, 1).start()
        part_copy(half + at, up, 0).start()
        return 0

    lax.fori_loop(0, half, two_direct, 0)

    def one_relay(at, target, origin, side):
        relay_copy(at, far, origin).wait_recv()
        joined = own_part[at, target] + relay_in[at].astype(jnp.float32)
        parts_out[at, target] = joined.astype(jnp.bfloat16)
        part_copy(at, target, side).start()

    def two_relays(at, _):
        one_relay(at, up, down, 0)
        one_relay(half + at, down, up, 1)
        return 0

    lax.fori_loop(0, half, two_relays, 0)

    lax.fori_loop(max(1, shards - LAG), shards, one_return, 0)
    for head in range(heads):
        cols = slice(head * HD, (head + 1) * HD)
        for block in range(blocks):
            rows = slice(block * BLOCK, (block + 1) * BLOCK)
            both = sums_here[head * blocks + block].astype(jnp.bfloat16)
            dk[rows, cols] = both[:, :HD]
            dv[rows, cols] = both[:, HD:]

    def one_sum(at, _):
        row_sum = own_part[at, lane]
        for side, target in ((0, up), (1, down)):
            part_copy(at, target, side).wait()
            row_sum += parts_in[at, side].astype(jnp.float32)
        relay_copy(at, far, up).wait_send()
        columns = pl.ds(pl.multiple_of(at * piece, piece), piece)
        x_grad[:, columns] = row_sum.astype(jnp.bfloat16)
        return 0

    lax.fori_loop(0, pieces, one_sum, 0)

    lax.fori_loop(max(1, shards - WINDOW), shards, sent_step, 0)

    def finish_requester(source, _):
        back_copy(source, source, source, source).wait_send()
        ask_copy(asked, source, source, source, source).wait_send()
        return 0

    lax.fori_loop(0, me, finish_requester, 0)


def hand_out_kernel(*refs):
    for given, result in zip(refs[:3], refs[3:]):
        result[...] = given[...]


HELD = pl.BlockSpec(memory_space=pl.ANY)
VMEM = pl.BlockSpec(memory_space=pltpu.VMEM)


def per_device(queries, keys, values, outputs, out_grad, log_sum, selected, w_query):
    tokens, width = queries.shape
    heads, blocks, _ = selected.shape
    shards = lax.axis_size("seq")
    result = jax.ShapeDtypeStruct((tokens, width), jnp.bfloat16)
    paired = (shards, CAP, BLOCK, 2 * HD)
    lanes_all = lax.axis_size("head")
    stripe = tokens // lanes_all
    width_in = w_query.shape[0]
    piece = min(512, width_in // 2)
    pieces = width_in // piece
    split = (pieces, lanes_all, stripe, piece)
    arrays = pl.pallas_call(
        exchange_kernel,
        out_shape=(
            jax.ShapeDtypeStruct((stripe, width_in), jnp.bfloat16),
            result,
            result,
        ),
        in_specs=[VMEM] + [HELD] * 5 + [VMEM, HELD],
        out_specs=(VMEM,) * 3,
        scratch_shapes=[pltpu.VMEM((tokens, width), jnp.bfloat16)] * 5
        + [
            pltpu.VMEM((heads, 1, tokens), jnp.float32),
            pltpu.VMEM((heads, 1, tokens), jnp.float32),
            pltpu.VMEM((heads * blocks, BLOCK, 2 * HD), jnp.float32),
            pltpu.VMEM(paired, jnp.bfloat16),
            pltpu.VMEM((shards, 1, HD), jnp.int32),
            pltpu.VMEM((shards, 1, HD), jnp.int32),
            pltpu.VMEM(paired, jnp.bfloat16),
            pltpu.VMEM((heads * blocks, BLOCK, 2 * HD), jnp.bfloat16),
            pltpu.SMEM((shards, 1, HD), jnp.int32),
            pltpu.SMEM((shards, 1, HD), jnp.int32),
            pltpu.VMEM((shards, 1, HD), jnp.int32),
            pltpu.VMEM((8 + heads, HD), jnp.int32),
            pltpu.SMEM((8 + heads, HD), jnp.int32),
            pltpu.VMEM(paired, jnp.bfloat16),
            pltpu.VMEM(paired, jnp.bfloat16),
            pltpu.VMEM((heads, HD, tokens), jnp.float32),
            pltpu.VMEM((heads, tokens, HD), jnp.bfloat16),
            pltpu.VMEM((heads, tokens, HD), jnp.bfloat16),
            pltpu.VMEM((width_in, width), jnp.bfloat16),
            pltpu.VMEM((tokens, width), jnp.bfloat16),
            pltpu.VMEM(split, jnp.bfloat16),
            pltpu.VMEM((pieces, 2, stripe, piece), jnp.bfloat16),
            pltpu.VMEM((pieces, stripe, piece), jnp.bfloat16),
            pltpu.VMEM(split, jnp.float32),
        ]
        + [pltpu.SemaphoreType.DMA((shards,))] * 4
        + [pltpu.SemaphoreType.DMA((pieces, lanes_all)), pltpu.SemaphoreType.DMA((pieces, 2))]
        + [pltpu.SemaphoreType.DMA((pieces,))]
        + [pltpu.SemaphoreType.DMA((shards,))] * 2
        + [pltpu.SemaphoreType.DMA] * 3
        + [pltpu.SemaphoreType.DMA((5,)), pltpu.SemaphoreType.DMA],
        compiler_params=pltpu.CompilerParams(
            vmem_limit_bytes=56 * 2**20, collective_id=0, has_side_effects=True
        ),
        name="exchange",
    )(
        selected,
        queries,
        keys,
        values,
        outputs,
        out_grad,
        log_sum,
        w_query,
    )
    return pl.pallas_call(
        hand_out_kernel,
        out_shape=tuple(jax.ShapeDtypeStruct(a.shape, a.dtype) for a in arrays),
        in_specs=[VMEM] * 3,
        out_specs=(VMEM,) * 3,
        name="hand_out",
    )(*arrays)


def solution(mesh):
    in_specs = (P("seq", "head"),) * 5 + (P("head", "seq"), P("head", "seq", None), P(None, "head"))
    out_specs = (P(("seq", "head"), None), P("seq", "head"), P("seq", "head"))
    return jax.shard_map(
        per_device, mesh=mesh, in_specs=in_specs, out_specs=out_specs, check_vma=False
    )
```
